256 devices in a mesh: tm: 16 (over y, z_hi), space: 16 (over x, z_lo, core).
Axes of the slice: x: 4, y: 4, z: 8 (z_hi: 4, z_lo: 2; z = z_hi * 2 + z_lo), core: 2. Of those that a mesh axis runs over, the one named last changes fastest.
Arguments:
- tokens: bfloat16 [32, 16, 4, 49, 1408], P('tm', 'space'), may hold values from -6 to 6
- tile_of_slot: int32 [16], replicated, may hold values from 0 to 15, each once
- shifts: int32 [4, 2], replicated, may hold values from 0 to 13
- norm_gain_space: float32 [1408], replicated, may hold values from 0.1 to 1.9
- norm_bias_space: float32 [1408], replicated, may hold values from -3 to 3
- w_qkv_space: bfloat16 [1408, 3168], P('tm'), may hold values from -0.15625 to 0.15625
- w_out_space: bfloat16 [1056, 1408], P(None, 'tm'), may hold values from -0.1875 to 0.1875
- norm_gain_time: float32 [1408], replicated, may hold values from 0.1 to 1.9
- norm_bias_time: float32 [1408], replicated, may hold values from -3 to 3
- w_qkv_time: bfloat16 [1408, 3168], P('tm'), may hold values from -0.15625 to 0.15625
- w_out_time: bfloat16 [1056, 1408], P(None, 'tm'), may hold values from -0.1875 to 0.1875
Outputs:
- encoded: bfloat16 [32, 16, 4, 49, 1408], P('tm', 'space')
The draws below stay inside these ranges and needn't reach their ends.
Inputs may be any that keep to these rules, and one draw needn't show every extreme that they name: `tile_of_slot`: each of the 16 tiles is held by exactly one slot. `shifts`: offsets of a video's cyclic window shift, rows first.
All inputs are finite; a program needn't handle non-finite values.
Results may differ from the reference program's by a relative error of at most 0.012.
Values may be sent and summed in bfloat16 or wider, within the bound.
A program may use at most 128 MiB of HBM per device.

```python
import jax
import jax.numpy as jnp
from jax import lax

D = 1408
HEADS = 12
HEAD_DIM = 88
VIDEOS = 4
TILE = 7
E = 1056
TILE_TOKENS = 49
WINDOW = 14
TILES_SIDE = 4
TILES = 16
FRAME = 28
TIMES = 32


def touch_ends(result, key, least, largest):
    index_at = [jax.random.randint(jax.random.fold_in(key, axis), (), 0, length) for axis, length in enumerate(result.shape)]
    main_axis = result.shape.index(max(result.shape))
    neighbour = index_at[:main_axis] + [(index_at[main_axis] + 1) % result.shape[main_axis]] + index_at[main_axis + 1:]
    return result.at[tuple(index_at)].set(least).at[tuple(neighbour)].set(largest)


def levels(key, dims, shards, low, top_value):
    gain, own = 1.0, jax.random.fold_in(key, 6)
    for position, parts in shards:
        steps = jnp.exp(jax.random.uniform(jax.random.fold_in(own, position), (parts,), jnp.float32, low / len(shards), top_value / len(shards)))
        gain = gain * jnp.repeat(steps, dims[position] // parts).reshape([-1 if axis == position else 1 for axis in range(len(dims))])
    return gain


def scatter_about(rng, dims, scale, bound, shards=(), held_as=jnp.bfloat16):
    values = jax.random.normal(rng, dims, jnp.float32) * scale
    if len(shards) > 0:
        values = levels(rng, dims, shards, -0.22, 0.18) * values
    return jnp.clip(values, min=-bound, max=bound).astype(held_as)


def setup_inputs(seed: int = 0) -> dict:
    arg_keys = jax.random.split(jax.random.key(seed), 12)
    return {
        "tokens": scatter_about(arg_keys[0], (TIMES, TILES, VIDEOS, TILE_TOKENS, D), 1.0, 6.0, ((0, 16), (1, 16))),
        "tile_of_slot": jax.random.permutation(arg_keys[1], TILES).astype(jnp.int32),
        "shifts": touch_ends(jax.random.randint(arg_keys[2], (VIDEOS, 2), 0, WINDOW), jax.random.fold_in(arg_keys[2], 1), 0, WINDOW - 1).astype(jnp.int32),
        "norm_gain_space": jnp.clip(1.0 + 0.18 * jax.random.normal(arg_keys[3], (D,), jnp.float32), 0.1, 1.9),
        "norm_bias_space": scatter_about(arg_keys[4], (D,), 0.5, 3.0, (), jnp.float32),
        "w_qkv_space": scatter_about(arg_keys[5], (D, 3 * E), D ** -0.5, 0.15625, ((0, 16),)),
        "w_out_space": scatter_about(arg_keys[6], (E, D), E ** -0.5, 0.1875, ((1, 16),)),
        "norm_gain_time": jnp.clip(1.0 + 0.18 * jax.random.normal(arg_keys[7], (D,), jnp.float32), 0.1, 1.9),
        "norm_bias_time": scatter_about(arg_keys[8], (D,), 0.5, 3.0, (), jnp.float32),
        "w_qkv_time": scatter_about(arg_keys[9], (D, 3 * E), D ** -0.5, 0.15625, ((0, 16),)),
        "w_out_time": scatter_about(arg_keys[10], (E, D), E ** -0.5, 0.1875, ((1, 16),)),
    }


EPSILON = 1e-06

def layer_norm(values, norm_gain, norm_bias):
    widened = values.astype(jnp.float32)
    average = lax.optimization_barrier(jnp.mean(widened, axis=-1, keepdims=True))
    centered = widened - average
    variance = lax.optimization_barrier(jnp.mean(centered * centered, axis=-1, keepdims=True))
    return (centered * lax.rsqrt(variance + EPSILON) * norm_gain + norm_bias).astype(jnp.bfloat16)

def project(values, weight):
    flattened = values.reshape(-1, values.shape[-1])
    return jnp.dot(flattened, weight, preferred_element_type=jnp.float32).reshape(values.shape[:-1] + (weight.shape[1],))

def window_attend(frame_cells, offsets):
    frame_side = frame_cells.shape[0]
    per_side = frame_side // WINDOW
    places = jnp.arange(frame_side, dtype=jnp.int32)
    row_index = (places + offsets[0]) % frame_side
    col_index = (places + offsets[1]) % frame_side
    rolled = jnp.take(jnp.take(frame_cells, row_index, axis=0), col_index, axis=1)
    pieces = rolled.reshape(per_side, WINDOW, per_side, WINDOW, 3, HEADS, HEAD_DIM)
    pieces = pieces.transpose(4, 0, 2, 5, 1, 3, 6).reshape(3, per_side * per_side, HEADS, WINDOW * WINDOW, HEAD_DIM)
    row_part = (places >= frame_side - offsets[0]).astype(jnp.int32)
    col_part = (places >= frame_side - offsets[1]).astype(jnp.int32)
    region = (2 * row_part[:, None] + col_part[None, :]).reshape(per_side, WINDOW, per_side, WINDOW)
    region = region.transpose(0, 2, 1, 3).reshape(per_side * per_side, WINDOW * WINDOW)
    allowed = region[:, :, None] == region[:, None, :]
    queries = pieces[0].astype(jnp.float32)
    key_rows = pieces[1].astype(jnp.float32)
    values = pieces[2].astype(jnp.float32)
    scores = jnp.einsum('whqd,whkd->whqk', queries, key_rows) * HEAD_DIM ** (-0.5)
    weights = jnp.where(allowed[:, None], jnp.exp(scores), jnp.float32(0.0))
    shares = (weights / lax.optimization_barrier(jnp.sum(weights, axis=-1, keepdims=True))).astype(jnp.bfloat16)
    attended = jnp.einsum('whqk,whkd->whqd', shares.astype(jnp.float32), values).astype(jnp.bfloat16)
    attended = attended.reshape(per_side, per_side, HEADS, WINDOW, WINDOW, HEAD_DIM)
    attended = attended.transpose(0, 3, 1, 4, 2, 5).reshape(frame_side, frame_side, HEADS * HEAD_DIM)
    back_rows = (places - offsets[0]) % frame_side
    back_cols = (places - offsets[1]) % frame_side
    return jnp.take(jnp.take(attended, back_rows, axis=0), back_cols, axis=1)

def time_attend(packed):
    leading = packed.shape[:-1]
    pieces = packed.reshape(leading[0], -1, 3, HEADS, HEAD_DIM)
    queries = pieces[:, :, 0].astype(jnp.float32)
    key_rows = pieces[:, :, 1].astype(jnp.float32)
    values = pieces[:, :, 2].astype(jnp.float32)
    scores = jnp.einsum('tmhd,umhd->mhtu', queries, key_rows) * HEAD_DIM ** (-0.5)
    weights = jnp.exp(scores)
    shares = (weights / lax.optimization_barrier(jnp.sum(weights, axis=-1, keepdims=True))).astype(jnp.bfloat16)
    attended = jnp.einsum('mhtu,umhd->tmhd', shares.astype(jnp.float32), values).astype(jnp.bfloat16)
    return attended.reshape(leading + (HEADS * HEAD_DIM,))

def to_grid(values, inverse):
    steps, slot_count, videos, per_tile, columns = values.shape
    tile_grid = jnp.take(values, inverse, axis=1).reshape(steps, TILES_SIDE, TILES_SIDE, videos, TILE, TILE, columns)
    return tile_grid.transpose(0, 3, 1, 4, 2, 5, 6).reshape(steps, videos, FRAME, FRAME, columns)

def from_grid(values, tile_of_slot):
    steps, videos, frame_side, other_side, columns = values.shape
    tile_grid = values.reshape(steps, videos, TILES_SIDE, TILE, TILES_SIDE, TILE, columns)
    tile_grid = tile_grid.transpose(0, 2, 4, 1, 3, 5, 6).reshape(steps, TILES, videos, TILE * TILE, columns)
    return jnp.take(tile_grid, tile_of_slot, axis=1)

def reference(tokens, tile_of_slot, shifts, norm_gain_space, norm_bias_space, w_qkv_space, w_out_space, norm_gain_time, norm_bias_time, w_qkv_time, w_out_time):
    inverse = jnp.argsort(tile_of_slot).astype(jnp.int32)
    normed = layer_norm(tokens, norm_gain_space, norm_bias_space)
    projected = project(normed, w_qkv_space).astype(jnp.bfloat16)
    frames = to_grid(projected, inverse)
    attended = lax.map(lambda per_time: jax.vmap(window_attend)(per_time, shifts), frames)
    attended = from_grid(attended, tile_of_slot)
    middle = (tokens.astype(jnp.float32) + project(attended, w_out_space)).astype(jnp.bfloat16)
    normed = layer_norm(middle, norm_gain_time, norm_bias_time)
    projected = project(normed, w_qkv_time).astype(jnp.bfloat16)
    attended = lax.map(time_attend, jnp.moveaxis(projected, 1, 0))
    attended = jnp.moveaxis(attended, 0, 1)
    return (middle.astype(jnp.float32) + project(attended, w_out_time)).astype(jnp.bfloat16)
```

```python
import functools

import jax
import jax.numpy as jnp
from jax import lax
from jax.experimental import pallas as pl
from jax.experimental.pallas import tpu as pltpu
from jax.sharding import PartitionSpec as P

HEADS = 12
HEAD_DIM = 88
D = 1408
E = 1056
EP = 1152
WIN = 208
ROWS = 2 * WIN
POS = 13
TROWS = POS * 32
EPSILON = 1e-06
SCALE = HEAD_DIM ** (-0.5)
MESH = pl.DeviceIdType.MESH
F32 = jnp.float32
BF16 = jnp.bfloat16
COPIES = 72


def div(values, by):
    return lax.shift_right_logical(values * (-(-65536 // by)), 16)


def mod(values, by):
    return values - by * div(values, by)


def wrap(values, size):
    return values - jnp.where(values >= size, size, 0)


def iota(shape, axis):
    return lax.broadcasted_iota(jnp.int32, shape, axis)


def one_hot(index, columns):
    hit = index == iota((index.shape[0], columns), 1)
    return jnp.where(hit, F32(1.0), F32(0.0)).astype(BF16)


def matmul(left, right):
    return jnp.dot(left, right, preferred_element_type=F32)


def matmul_nt(left, right):
    return lax.dot_general(left, right, (((1,), (1,)), ((), ())), preferred_element_type=F32)


def tiles(width, step, do):
    whole = width // step

    def one(n, carry):
        do(pl.ds(pl.multiple_of(n * step, step), step))
        return carry

    lax.fori_loop(0, whole, one, 0)
    if width % step:
        do(pl.ds(whole * step, width % step))


def normalize(source, target, gain_ref, bias_ref, valid):
    def one(n, carry):
        rows = pl.ds(pl.multiple_of(n * 32, 32), 32)
        widened = source[rows, :].astype(F32)
        average = jnp.mean(widened, axis=-1, keepdims=True)
        centered = widened - average
        variance = jnp.mean(centered * centered, axis=-1, keepdims=True)
        normed = centered * lax.rsqrt(variance + EPSILON) * gain_ref[...] + bias_ref[...]
        keep = valid(n * 32 + iota((32, 1), 0))
        target[rows, :] = jnp.where(keep, normed, F32(0.0)).astype(BF16)
        return carry

    lax.fori_loop(0, ROWS // 32, one, 0)


def project(normed, full, qkv):
    def one(kind, carry):
        def tile(columns):
            qkv[kind, :, columns] = matmul(normed[...], full[kind, :, columns]).astype(BF16)

        tiles(EP, 256, tile)
        return carry

    lax.fori_loop(0, 3, one, 0)


def attend(qkv, mix, rows, allowed):
    count = allowed.shape[0]
    for head in range(HEADS):
        low = HEAD_DIM * head
        first = low // 128 * 128
        last = -(-(low + HEAD_DIM) // 128) * 128
        lane = first + iota((count, last - first), 1)
        own = (lane >= low) & (lane < low + HEAD_DIM)
        zero = jnp.zeros((count, last - first), BF16)
        query = qkv[0, rows, first:last]
        keys = jnp.where(own, qkv[1, rows, first:last], zero)
        values = jnp.where(own, qkv[2, rows, first:last], zero)
        weights = jnp.where(allowed, jnp.exp(matmul_nt(query, keys) * SCALE), F32(0.0))
        total = jnp.sum(weights, axis=-1, keepdims=True)
        shares = (weights * (1.0 / total)).astype(BF16)
        mixed = matmul(shares, values).astype(BF16)
        if low % 128 == 0:
            mix[rows, first:last] = mixed
        else:
            mix[rows, first : first + 128] = mix[rows, first : first + 128] + mixed[:, :128]
            if last - first > 128:
                mix[rows, first + 128 : last] = mixed[:, 128:]


def out_project(mix, full, residual, store):
    def tile(columns):
        product = matmul_nt(mix[...], full[3, columns, :])
        store(columns, (residual[:, columns].astype(F32) + product).astype(BF16))

    tiles(D, 256, tile)


def gather_steps(place, shard, zbuf, full, z_send, z_recv, z_local, send_sem, recv_sem, pending):
    y, zh, x, zl, c = place
    dev = device
    core_of = lax.div(zh, 2)
    is_sender = core_of == c
    mine = lax.rem(zh, 2)

    def z_copy(step):
        return pltpu.make_async_remote_copy(
            src_ref=shard.at[x],
            dst_ref=zbuf.at[mine],
            send_sem=z_send.at[step - 1],
            recv_sem=z_recv.at[mine],
            device_id=dev(y, lax.rem(zh + step, 4), x, zl, c),
            device_id_type=MESH,
        )

    def z_own():
        return pltpu.make_async_copy(shard.at[x], zbuf.at[mine], z_local)

    @pl.when(is_sender)
    def _():
        for step in (1, 3, 2):
            z_copy(step).start()
        z_own().start()

    def z_finish():
        @pl.when(is_sender)
        def _():
            for step in (1, 3, 2):
                z_copy(step).wait_send()

    pending.append(z_finish)
    yield

    for k in range(2):
        @pl.when(zh != 2 * c + k)
        def _():
            pltpu.make_async_remote_copy(
                src_ref=shard.at[x],
                dst_ref=zbuf.at[k],
                send_sem=z_send.at[0],
                recv_sem=z_recv.at[k],
                device_id=dev(y, zh, x, zl, 1 - c),
                device_id_type=MESH,
            ).wait_recv()

    @pl.when(is_sender)
    def _():
        z_own().wait()

    def region(kind, row, core, low, count):
        start = pl.multiple_of(352 * lax.rem(y + row + 4, 4) + 176 * core + low, 16)
        return full.at[lax.rem(x + kind + 4, 4), pl.ds(start, count), :]

    base = pl.multiple_of(352 * y + 176 * c, 16)
    both = jnp.concatenate([zbuf[0].astype(F32), zbuf[1].astype(F32)], axis=0)
    full[x, pl.ds(base, 176), :] = both.astype(BF16)

    xp, xm = dev(y, zh, lax.rem(x + 1, 4), zl, c), dev(y, zh, lax.rem(x + 3, 4), zl, c)
    yp, ym = dev(lax.rem(y + 1, 4), zh, x, zl, c), dev(lax.rem(y + 3, 4), zh, x, zl, c)
    sibling = dev(y, zh, x, zl, 1 - c)
    counter = [0]

    def copy(k, piece, target):
        return pltpu.make_async_remote_copy(
            src_ref=piece,
            dst_ref=piece,
            send_sem=send_sem.at[k],
            recv_sem=recv_sem.at[k],
            device_id=target,
            device_id_type=MESH,
        )

    def send(piece, target):
        k = counter[0]
        counter[0] += 1
        made = copy(k, piece, target)
        made.start()
        pending.append(made.wait_send)
        return k

    def recv(k, piece):
        copy(k, piece, sibling).wait_recv()

    def part_a(kind, row, low=0, count=96, core=c):
        return region(kind, row, core, low, count)

    def part_b(kind, row, low=0, count=80, core=c):
        return region(kind, row, core, 96 + low, count)

    arriving = []

    def share(part, kind, row):
        arriving.append((send(part(kind, row), sibling), part(kind, row, core=1 - c)))

    class Ring:
        def __init__(self, part, along_x, at, plus, minus, halves):
            self.part, self.along_x, self.at = part, along_x, at
            self.plus, self.minus, self.halves = plus, minus, halves
            own = self.piece(0)
            self.k_plus = send(own, plus)
            self.k_minus = send(own, minus)

        def spot(self, step):
            return (step, self.at) if self.along_x else (self.at, step)

        def piece(self, step, *cut):
            return self.part(*self.spot(step), *cut)

        def near(self):
            low, high = self.halves
            recv(self.k_plus, self.piece(-1))
            self.f_plus = send(self.piece(-1, 0, low), self.plus)
            recv(self.k_minus, self.piece(1))
            self.f_minus = send(self.piece(1, low, high), self.minus)

        def far(self):
            low, high = self.halves
            recv(self.f_plus, self.piece(2, 0, low))
            recv(self.f_minus, self.piece(2, low, high))

    def ring_a1():
        return Ring(part_a, True, 0, xp, xm, (48, 48))

    def ring_b1():
        return Ring(part_b, False, 0, yp, ym, (48, 32))

    def ring_a2(kind):
        return Ring(part_a, False, kind, yp, ym, (48, 48))

    def ring_b2(row):
        return Ring(part_b, True, row, xp, xm, (48, 32))

    a1, b1 = ring_a1(), ring_b1()
    seconds = [ring_a2(0), ring_b2(0)]
    share(part_a, 0, 0)
    share(part_b, 0, 0)
    yield
    a1.near()
    b1.near()
    for step in (-1, 1):
        seconds += [ring_a2(step), ring_b2(step)]
    for step in (-1, 1):
        share(part_a, step, 0)
        share(part_b, 0, step)
    yield
    a1.far()
    b1.far()
    seconds += [ring_a2(2), ring_b2(2)]
    share(part_a, 2, 0)
    share(part_b, 0, 2)
    for ring in seconds[:4]:
        ring.near()
        for step in (-1, 1):
            share(ring.part, *ring.spot(step))
    yield
    for ring in seconds[4:]:
        ring.near()
        for step in (-1, 1):
            share(ring.part, *ring.spot(step))
    for ring in seconds[:4]:
        ring.far()
        share(ring.part, *ring.spot(2))
    yield
    for ring in seconds[4:]:
        ring.far()
        share(ring.part, *ring.spot(2))
    for k, piece in arriving:
        recv(k, piece)
    assert counter[0] == COPIES, counter
    yield


def device(y, zh, x, zl, c):
    return (y * 4 + zh, x * 4 + zl * 2 + c)


def advance(steps):
    next(steps, None)


def kernel(
    slots, shifts, tokens, shard1, shard2, gain1, bias1, gain2, bias2, out,
    full1, full2, zbuf1, zbuf2, frames, p_in, p_out, xw, xn, qkv, mix, mid2, snd, rbuf, ret, obuf,
    z_send, z_recv, z_local, g_send, g_recv, e1_send, e1_recv, e1_local, m_sem,
    e2_send, e2_recv, e2_local, e3_send, e3_recv, e3_local,
):
    tm, space = lax.axis_index("tm"), lax.axis_index("space")
    y, zh = lax.div(tm, 4), lax.rem(tm, 4)
    x, zl, c = lax.div(space, 4), lax.rem(lax.div(space, 2), 2), lax.rem(space, 2)
    place = (y, zh, x, zl, c)
    sibling = device(y, zh, x, zl, 1 - c)
    video_t = lax.rem(zh - y + 4, 4)
    is_self = video_t == x
    pending = []

    barrier = pltpu.get_barrier_semaphore()

    def greet(target):
        pl.semaphore_signal(barrier, inc=1, device_id=target, device_id_type=MESH)

    greet(sibling)
    for step in range(1, 8):
        greet(device(y, zh, lax.rem(x + step // 2, 4), lax.rem(zl + step % 2, 2), c))

    def greet_times(n, carry):
        other = lax.rem(tm + n, 16)
        greet((other, space))
        return carry

    lax.fori_loop(1, 16, greet_times, 0)

    def greet_sources(n, carry):
        other = lax.rem(tm + lax.div(n, 2), 16)
        zl_other = lax.rem(zl + lax.rem(n, 2), 2)

        @pl.when(jnp.logical_not(is_self & (n == 0)))
        def _():
            greet((other, video_t * 4 + zl_other * 2 + c))

        return carry

    lax.fori_loop(0, 32, greet_sources, 0)
    pl.semaphore_wait(barrier, 55 - jnp.where(is_self, 1, 0))

    g1 = gather_steps(
        place, shard1, zbuf1, full1, z_send.at[0], z_recv.at[0], z_local.at[0],
        g_send.at[0], g_recv.at[0], pending,
    )
    g2 = gather_steps(
        place, shard2, zbuf2, full2, z_send.at[1], z_recv.at[1], z_local.at[1],
        g_send.at[1], g_recv.at[1], pending,
    )
    advance(g1)

    own_tile = pltpu.make_async_copy(tokens.at[zl * 4 + x], frames.at[space], e1_local)
    own_tile.start()
    for n, step in enumerate((2, 6, 1, 3, 7, 4, 5)):
        xo, zo = lax.rem(x + step // 2, 4), lax.rem(zl + step % 2, 2)
        made = pltpu.make_async_remote_copy(
            src_ref=tokens.at[zo * 4 + xo],
            dst_ref=frames.at[space],
            send_sem=e1_send.at[n],
            recv_sem=e1_recv.at[space],
            device_id=device(y, zh, xo, zo, c),
            device_id_type=MESH,
        )
        made.start()
        pending.append(made.wait_send)

    shift_r, shift_c = shifts[x, 0], shifts[x, 1]

    row = iota((ROWS, 1), 0)
    wc = div(row, WIN)
    spot = row - wc * WIN
    pr = div(spot, 14)
    pc = spot - 14 * pr
    r = wrap(14 * c + pr + shift_r, 28)
    col = wrap(14 * wc + pc + shift_c, 28)
    tile = 4 * div(r, 7) + div(col, 7)
    slot = jnp.zeros_like(tile)
    for s in range(16):
        slot = jnp.where(tile == slots[s], s, slot)
    index = slot * 64 + mod(r, 7) * 7 + mod(col, 7)
    p_in[...] = one_hot(jnp.where(spot < 196, index, -1), 1024)

    advance(g1)

    row = iota((512, 1), 0)
    slot8 = div(row, 64)
    p = mod(row, 16)
    j = POS * mod(div(row, 16), 4) + p
    tile = jnp.zeros_like(row)
    for n in range(8):
        tile = jnp.where(slot8 == n, slots[4 * (n // 2) + 2 * (n % 2) + c], tile)
    jr = div(j, 7)
    r = 7 * div(tile, 4) + jr
    col = 7 * mod(tile, 4) + (j - 7 * jr)
    sr = wrap(r + 28 - shift_r, 28)
    sc = wrap(col + 28 - shift_c, 28)
    wr, wc = div(sr, 14), div(sc, 14)
    index = wr * ROWS + wc * WIN + (sr - 14 * wr) * 14 + (sc - 14 * wc)
    p_out[...] = one_hot(jnp.where((p < POS) & (j < 49), index, -1), 2 * ROWS)

    own_tile.wait()

    def tile_copy(s, n):
        return pltpu.make_async_remote_copy(
            src_ref=frames.at[s],
            dst_ref=frames.at[s],
            send_sem=e1_send.at[7 + n],
            recv_sem=e1_recv.at[s],
            device_id=sibling,
            device_id_type=MESH,
        )

    for n, step in enumerate((0, 2, 6, 1, 3, 7, 4, 5)):
        xo, zo = lax.rem(x + step // 2, 4), lax.rem(zl + step % 2, 2)
        s = xo * 4 + zo * 2 + c
        made = tile_copy(s, n)
        if step:
            made.wait_recv()
        made.start()
        pending.append(made.wait_send)
    advance(g1)
    for step in range(8):
        s = 4 * (step // 2) + 2 * (step % 2) + 1 - c
        tile_copy(s, 0).wait_recv()

    def pick(columns):
        cells = frames[:, :, columns]
        cells = cells.reshape(1024, cells.shape[2])
        xw[:, columns] = matmul(p_in[...], cells).astype(BF16)

    tiles(D, 256, pick)

    def in_window(rows):
        return rows - jnp.where(rows >= WIN, WIN, 0) < 196

    normalize(xw, xn, gain1, bias1, in_window)
    advance(g1)
    advance(g1)
    advance(g1)
    advance(g2)
    project(xn, full1, qkv)
    advance(g2)

    def regions(shape, axis, column):
        at = iota(shape, axis)
        down = div(at, 14)
        across = at - 14 * down
        kind = 2 * jnp.where(14 * c + down >= 28 - shift_r, 1, 0)
        kind = kind + jnp.where(14 * column + across >= 28 - shift_c, 1, 0)
        return jnp.where(at < 196, kind, -1)

    for column in range(2):
        allowed = regions((WIN, 1), 0, column) == regions((1, WIN), 1, column)
        attend(qkv, mix, pl.ds(column * WIN, WIN), allowed)
        advance(g2)

    def keep_middle(columns, values):
        mid2[c, :, columns] = values

    out_project(mix, full1, xw, keep_middle)

    swap = pltpu.make_async_remote_copy(
        src_ref=mid2.at[c],
        dst_ref=mid2.at[c],
        send_sem=m_sem.at[0],
        recv_sem=m_sem.at[1],
        device_id=sibling,
        device_id_type=MESH,
    )
    swap.start()
    pending.append(swap.wait_send)
    pltpu.make_async_remote_copy(
        src_ref=mid2.at[1 - c],
        dst_ref=mid2.at[1 - c],
        send_sem=m_sem.at[0],
        recv_sem=m_sem.at[1],
        device_id=sibling,
        device_id_type=MESH,
    ).wait_recv()

    def spread(columns):
        cells = mid2[:, :, columns]
        width = cells.shape[2]
        moved = matmul(p_out[...], cells.reshape(2 * ROWS, width)).astype(BF16)
        snd[:, :, columns] = moved.reshape(32, 16, width)

    tiles(D, 256, spread)

    time = 2 * tm + zl

    def row_copy(n):
        dx, dz, dq = lax.div(n, 8), lax.rem(lax.div(n, 4), 2), lax.rem(n, 4)
        xo, zo, q = lax.rem(x + dx, 4), lax.rem(zl + dz, 2), lax.rem(y + dq, 4)
        return pltpu.make_async_remote_copy(
            src_ref=snd.at[(xo * 2 + zo) * 4 + q],
            dst_ref=rbuf.at[time],
            send_sem=e2_send.at[n],
            recv_sem=e2_recv.at[time],
            device_id=device(q, lax.rem(q + x, 4), xo, zo, c),
            device_id_type=MESH,
        )

    own_rows = pltpu.make_async_copy(snd.at[(x * 2 + zl) * 4 + y], rbuf.at[time], e2_local)

    def start_rows(n, carry):
        @pl.when(jnp.logical_not(is_self & (n == 0)))
        def _():
            row_copy(n).start()

        return carry

    lax.fori_loop(0, 32, start_rows, 0)

    @pl.when(is_self)
    def _():
        own_rows.start()
        own_rows.wait()

    advance(g2)
    advance(g2)

    def wait_rows(n, carry):
        @pl.when(jnp.logical_not(is_self & (n == time)))
        def _():
            pltpu.make_async_remote_copy(
                src_ref=snd.at[0],
                dst_ref=rbuf.at[n],
                send_sem=e2_send.at[0],
                recv_sem=e2_recv.at[n],
                device_id=sibling,
                device_id_type=MESH,
            ).wait_recv()

        return carry

    lax.fori_loop(0, 32, wait_rows, 0)

    row = iota((TROWS, 1), 0)
    at = div(row, 32)
    by_position = one_hot((row - 32 * at) * 16 + at, 512)

    def turn(columns):
        cells = rbuf[:, :, columns]
        cells = cells.reshape(512, cells.shape[2])
        xw[:, columns] = matmul(by_position, cells).astype(BF16)

    tiles(D, 256, turn)
    normalize(xw, xn, gain2, bias2, lambda rows: div(rows, 32) + POS * y < 49)
    advance(g2)
    project(xn, full2, qkv)

    for first, count in ((0, 128), (128, 128), (256, 128), (384, 32)):
        left, right = iota((count, 1), 0), iota((1, count), 1)
        attend(qkv, mix, pl.ds(first, count), div(left, 32) == div(right, 32))

    def keep_encoded(columns, values):
        xn[:, columns] = values

    out_project(mix, full2, xw, keep_encoded)

    row = iota((512, 1), 0)
    at = div(row, 16)
    p = row - 16 * at
    by_time = one_hot(jnp.where(p < POS, p * 32 + at, -1), TROWS)

    def turn_back(columns):
        moved = matmul(by_time, xn[:, columns]).astype(BF16)
        ret[:, :, columns] = moved.reshape(32, 16, moved.shape[1])

    tiles(D, 256, turn_back)

    def back_copy(n):
        other = lax.rem(tm + n, 16)
        return pltpu.make_async_remote_copy(
            src_ref=ret.at[pl.ds(2 * other, 2)],
            dst_ref=obuf.at[tm],
            send_sem=e3_send.at[n],
            recv_sem=e3_recv.at[tm],
            device_id=(other, space),
            device_id_type=MESH,
        )

    def start_back(n, carry):
        back_copy(n).start()
        return carry

    lax.fori_loop(1, 16, start_back, 0)
    own_back = pltpu.make_async_copy(ret.at[pl.ds(2 * tm, 2)], obuf.at[tm], e3_local)
    own_back.start()
    own_back.wait()

    def wait_back(n, carry):
        other = lax.rem(tm + n, 16)
        pltpu.make_async_remote_copy(
            src_ref=obuf.at[other],
            dst_ref=obuf.at[other],
            send_sem=e3_send.at[0],
            recv_sem=e3_recv.at[other],
            device_id=sibling,
            device_id_type=MESH,
        ).wait_recv()
        return carry

    lax.fori_loop(1, 16, wait_back, 0)

    row = iota((64, 1), 0)
    q = div(row, POS)
    join = one_hot(jnp.where(row < 49, q * 16 + row - POS * q, -1), 64)
    for t in range(2):
        for v in range(4):
            parts = [obuf[4 * n + (n + v) % 4, t] for n in range(4)]
            whole = matmul(join, jnp.concatenate(parts, axis=0)).astype(BF16)
            out[t, v] = whole[:49]

    for finish in pending:
        finish()

    def finish_rows(n, carry):
        @pl.when(jnp.logical_not(is_self & (n == 0)))
        def _():
            row_copy(n).wait_send()

        return carry

    lax.fori_loop(0, 32, finish_rows, 0)

    def finish_back(n, carry):
        back_copy(n).wait_send()
        return carry

    lax.fori_loop(1, 16, finish_back, 0)


def stack_weights(w_qkv, w_out):
    rows = w_qkv.shape[0]
    kinds = w_qkv.reshape(rows, 3, E).transpose(1, 0, 2)
    return jnp.pad(jnp.concatenate([kinds, w_out.T[None]], axis=0), ((0, 0), (0, 0), (0, EP - E)))


def body(
    tokens, tile_of_slot, shifts, norm_gain_space, norm_bias_space, w_qkv_space, w_out_space,
    norm_gain_time, norm_bias_time, w_qkv_time, w_out_time,
):
    cells = jnp.pad(tokens.reshape(8, 49, D), ((0, 0), (0, 15), (0, 0)))
    smem = pl.BlockSpec(memory_space=pltpu.SMEM)
    vmem = pl.BlockSpec(memory_space=pltpu.VMEM)
    anywhere = pl.BlockSpec(memory_space=pl.ANY)
    dma = pltpu.SemaphoreType.DMA
    encoded = pl.pallas_call(
        kernel,
        out_shape=jax.ShapeDtypeStruct((2, 4, 49, D), BF16),
        in_specs=[smem, smem, anywhere, anywhere, anywhere, vmem, vmem, vmem, vmem],
        out_specs=vmem,
        scratch_shapes=[
            pltpu.VMEM((4, D, EP), BF16),
            pltpu.VMEM((4, D, EP), BF16),
            pltpu.VMEM((2, 88, EP), BF16),
            pltpu.VMEM((2, 88, EP), BF16),
            pltpu.VMEM((16, 64, D), BF16),
            pltpu.VMEM((ROWS, 1024), BF16),
            pltpu.VMEM((512, 2 * ROWS), BF16),
            pltpu.VMEM((ROWS, D), BF16),
            pltpu.VMEM((ROWS, D), BF16),
            pltpu.VMEM((3, ROWS, EP), BF16),
            pltpu.VMEM((ROWS, EP), BF16),
            pltpu.VMEM((2, ROWS, D), BF16),
            pltpu.VMEM((32, 16, D), BF16),
            pltpu.VMEM((32, 16, D), BF16),
            pltpu.VMEM((32, 16, D), BF16),
            pltpu.VMEM((16, 2, 16, D), BF16),
            dma((2, 3)), dma((2, 2)), dma((2,)), dma((2, COPIES)), dma((2, COPIES)),
            dma((15,)), dma((16,)), dma, dma((2,)),
            dma((32,)), dma((32,)), dma, dma((16,)), dma((16,)), dma,
        ],
        compiler_params=pltpu.CompilerParams(
            collective_id=0, has_side_effects=True, vmem_limit_bytes=60 * 1024 * 1024
        ),
        cost_estimate=pl.CostEstimate(flops=12_000_000_000, bytes_accessed=40_000_000, transcendentals=2_000_000),
    )(
        tile_of_slot, shifts, cells, stack_weights(w_qkv_space, w_out_space),
        stack_weights(w_qkv_time, w_out_time),
        norm_gain_space[None], norm_bias_space[None], norm_gain_time[None], norm_bias_time[None],
    )
    return encoded.reshape(tokens.shape)


def solution(mesh):
    placed = (
        P("tm", "space", None, None, None), P(), P(), P(), P(), P("tm", None), P(None, "tm"),
        P(), P(), P("tm", None), P(None, "tm"),
    )
    return jax.shard_map(
        body,
        mesh=mesh,
        in_specs=placed,
        out_specs=P("tm", "space", None, None, None),
        check_vma=False,
    )
```

```python
import functools

import jax
import jax.numpy as jnp
from jax import lax
from jax.experimental import pallas as pl
from jax.experimental.pallas import tpu as pltpu
from jax.sharding import PartitionSpec as P

HEADS = 12
HEAD_DIM = 88
D = 1408
E = 1056
EP = 1152
WIN = 208
ROWS = 2 * WIN
POS = 13
TROWS = POS * 32
EPSILON = 1e-06
SCALE = HEAD_DIM ** (-0.5)
MESH = pl.DeviceIdType.MESH
F32 = jnp.float32
BF16 = jnp.bfloat16
COPIES = (72, 72)
PARTS = ((0, 768), (768, 640))


def div(values, by):
    return lax.shift_right_logical(values * (-(-65536 // by)), 16)


def mod(values, by):
    return values - by * div(values, by)


def wrap(values, size):
    return values - jnp.where(values >= size, size, 0)


def iota(shape, axis):
    return lax.broadcasted_iota(jnp.int32, shape, axis)


def one_hot(index, columns):
    hit = index == iota((index.shape[0], columns), 1)
    return jnp.where(hit, F32(1.0), F32(0.0)).astype(BF16)


def matmul(left, right):
    return jnp.dot(left, right, preferred_element_type=F32)


def matmul_nt(left, right):
    return lax.dot_general(left, right, (((1,), (1,)), ((), ())), preferred_element_type=F32)


def normalize(source, target, gain_ref, bias_ref, valid):
    def one(n, carry):
        rows = pl.ds(pl.multiple_of(n * 32, 32), 32)
        widened = source[rows, :].astype(F32)
        average = jnp.mean(widened, axis=-1, keepdims=True)
        centered = widened - average
        variance = jnp.mean(centered * centered, axis=-1, keepdims=True)
        normed = centered * lax.rsqrt(variance + EPSILON) * gain_ref[...] + bias_ref[...]
        keep = valid(n * 32 + iota((32, 1), 0))
        target[rows, :] = jnp.where(keep, normed, F32(0.0)).astype(BF16)
        return carry

    lax.fori_loop(0, ROWS // 32, one, 0)


def project(normed, full, qkv, kind):
    qkv[kind] = matmul(normed[...], full[kind]).astype(BF16)


def attend(qkv, mix, rows, allowed):
    count = allowed.shape[0]
    for head in range(HEADS):
        low = HEAD_DIM * head
        first = low // 128 * 128
        last = -(-(low + HEAD_DIM) // 128) * 128
        lane = first + iota((count, last - first), 1)
        own = (lane >= low) & (lane < low + HEAD_DIM)
        zero = jnp.zeros((count, last - first), BF16)
        query = qkv[0, rows, first:last]
        keys = jnp.where(own, qkv[1, rows, first:last], zero)
        values = jnp.where(own, qkv[2, rows, first:last], zero)
        weights = jnp.where(allowed, jnp.exp(matmul_nt(query, keys) * SCALE), F32(0.0))
        total = jnp.sum(weights, axis=-1, keepdims=True)
        shares = (weights * (1.0 / total)).astype(BF16)
        mixed = matmul(shares, values).astype(BF16)
        if low % 128 == 0:
            mix[rows, first:last] = mixed
        else:
            mix[rows, first : first + 128] = mix[rows, first : first + 128] + mixed[:, :128]
            if last - first > 128:
                mix[rows, first + 128 : last] = mixed[:, 128:]


def out_project(mix, full, residual, columns):
    product = matmul_nt(mix[...], full[3, columns, :])
    return (residual[:, columns].astype(F32) + product).astype(BF16)


def stage_shard(place, w_qkv, w_out, staged):
    x = place[2]
    staged[...] = jnp.zeros_like(staged)
    for kind in range(3):
        @pl.when(x == kind)
        def _():
            staged[:, :E] = w_qkv[:, E * kind : E * kind + E]

    @pl.when(x == 3)
    def _():
        eye = one_hot(iota((88, 1), 0), 88)
        staged[:, :E] = matmul_nt(eye, w_out[...]).astype(BF16)


def gather_steps(place, sizes, staged, zbuf, full, z_send, z_recv, z_local, send_sem, recv_sem, pending):
    y, zh, x, zl, c = place
    dev = device
    core_of = lax.div(zh, 2)
    is_sender = core_of == c
    mine = lax.rem(zh, 2)

    def z_copy(step):
        return pltpu.make_async_remote_copy(
            src_ref=staged,
            dst_ref=zbuf.at[mine],
            send_sem=z_send.at[step - 1],
            recv_sem=z_recv.at[mine],
            device_id=dev(y, lax.rem(zh + step, 4), x, zl, c),
            device_id_type=MESH,
        )

    def z_own():
        return pltpu.make_async_copy(staged, zbuf.at[mine], z_local)

    @pl.when(is_sender)
    def _():
        for step in (1, 3, 2):
            z_copy(step).start()
        z_own().start()

    def z_finish():
        @pl.when(is_sender)
        def _():
            for step in (1, 3, 2):
                z_copy(step).wait_send()

    pending.append(z_finish)
    yield

    for k in range(2):
        @pl.when(zh != 2 * c + k)
        def _():
            pltpu.make_async_remote_copy(
                src_ref=staged,
                dst_ref=zbuf.at[k],
                send_sem=z_send.at[0],
                recv_sem=z_recv.at[k],
                device_id=dev(y, zh, x, zl, 1 - c),
                device_id_type=MESH,
            ).wait_recv()

    @pl.when(is_sender)
    def _():
        z_own().wait()

    def region(kind, row, core, low, count):
        start = pl.multiple_of(352 * lax.rem(y + row + 4, 4) + 176 * core + low, 16)
        return full.at[lax.rem(x + kind + 4, 4), pl.ds(start, count), :]

    rows_a, rows_b, split_z = sizes
    low_a = 80 * zl if split_z else 0
    low_b = 96 - 48 * zl if split_z else rows_a
    base = pl.multiple_of(352 * y + 176 * c, 16)
    both = jnp.concatenate([zbuf[0].astype(F32), zbuf[1].astype(F32)], axis=0)
    full[x, pl.ds(base, 176), :] = both.astype(BF16)

    xp, xm = dev(y, zh, lax.rem(x + 1, 4), zl, c), dev(y, zh, lax.rem(x + 3, 4), zl, c)
    yp, ym = dev(lax.rem(y + 1, 4), zh, x, zl, c), dev(lax.rem(y + 3, 4), zh, x, zl, c)
    sibling = dev(y, zh, x, zl, 1 - c)
    counter = [0]

    def copy(k, piece, target):
        return pltpu.make_async_remote_copy(
            src_ref=piece,
            dst_ref=piece,
            send_sem=send_sem.at[k],
            recv_sem=recv_sem.at[k],
            device_id=target,
            device_id_type=MESH,
        )

    def send(piece, target):
        k = counter[0]
        counter[0] += 1
        made = copy(k, piece, target)
        made.start()
        pending.append(made.wait_send)
        return k

    def recv(k, piece):
        copy(k, piece, sibling).wait_recv()

    def part_a(kind, row, low=0, count=rows_a, core=c):
        return region(kind, row, core, low_a + low, count)

    def part_b(kind, row, low=0, count=rows_b, core=c):
        return region(kind, row, core, low_b + low, count)

    def part_z(kind, row, parity, low=0, count=48, core=c):
        return region(kind, row, core, 128 * parity + low, count)

    arriving = []
    half_b = 16 * ((rows_b // 16 + 1) // 2)

    inner = dev(y, zh, x, 1 - zl, c)
    outer = dev(y, lax.rem(zh + 2 * zl + 3, 4), x, 1 - zl, c)
    crossing = []

    def share(part, kind, row):
        arriving.append((send(part(kind, row), sibling), part(kind, row, core=1 - c)))
        if not split_z or part is not part_a:
            return
        if kind == 0 and row == 0:
            k = send(part_z(0, 0, 1 - zl), sibling)
            arriving.append((k, part_z(0, 0, 1 - zl, core=1 - c)))
        else:
            k_out = send(part_z(kind, row, zl, 0, 32), outer)
            k_in = send(part_z(kind, row, zl, 32, 16), inner)
            crossing.append((kind, row, k_out, k_in))

    def crossed(count):
        for kind, row, k_out, k_in in crossing[:count]:
            recv(k_out, part_z(kind, row, 1 - zl, 0, 32))
            recv(k_in, part_z(kind, row, 1 - zl, 32, 16))
            k = send(part_z(kind, row, 1 - zl), sibling)
            arriving.append((k, part_z(kind, row, 1 - zl, core=1 - c)))
        del crossing[:count]

    class Ring:
        def __init__(self, part, along_x, at, plus, minus, halves):
            self.part, self.along_x, self.at = part, along_x, at
            self.plus, self.minus, self.halves = plus, minus, halves
            own = self.piece(0)
            self.k_plus = send(own, plus)
            self.k_minus = send(own, minus)

        def spot(self, step):
            return (step, self.at) if self.along_x else (self.at, step)

        def piece(self, step, *cut):
            return self.part(*self.spot(step), *cut)

        def near(self):
            low, high = self.halves
            recv(self.k_plus, self.piece(-1))
            self.f_plus = send(self.piece(-1, 0, low), self.plus)
            recv(self.k_minus, self.piece(1))
            self.f_minus = send(self.piece(1, low, high), self.minus)

        def far(self):
            low, high = self.halves
            recv(self.f_plus, self.piece(2, 0, low))
            recv(self.f_minus, self.piece(2, low, high))

    def ring_a1():
        return Ring(part_a, True, 0, xp, xm, (48, rows_a - 48))

    def ring_b1():
        return Ring(part_b, False, 0, yp, ym, (half_b, rows_b - half_b))

    def ring_a2(kind):
        return Ring(part_a, False, kind, yp, ym, (48, rows_a - 48))

    def ring_b2(row):
        return Ring(part_b, True, row, xp, xm, (half_b, rows_b - half_b))

    a1, b1 = ring_a1(), ring_b1()
    seconds = [ring_a2(0), ring_b2(0)]
    share(part_a, 0, 0)
    share(part_b, 0, 0)
    yield
    a1.near()
    b1.near()
    for step in (-1, 1):
        seconds += [ring_a2(step), ring_b2(step)]
    for step in (-1, 1):
        share(part_a, step, 0)
        share(part_b, 0, step)
    yield
    a1.far()
    b1.far()
    seconds += [ring_a2(2), ring_b2(2)]
    share(part_a, 2, 0)
    share(part_b, 0, 2)
    yield
    for n in range(0, 8, 2):
        for ring in seconds[n : n + 2]:
            ring.near()
            for step in (-1, 1):
                share(ring.part, *ring.spot(step))
        yield
    for n in range(0, 8, 2):
        for ring in seconds[n : n + 2]:
            ring.far()
            share(ring.part, *ring.spot(2))
        if n < 6:
            yield
    yield
    crossed(len(crossing))
    for k, piece in arriving:
        recv(k, piece)
    assert counter[0] == send_sem.shape[0], counter
    yield


def device(y, zh, x, zl, c):
    return (y * 4 + zh, x * 4 + zl * 2 + c)


def advance(steps):
    next(steps, None)


def kernel(
    slots, shifts, tokens, w_qkv1, w_out1, w_qkv2, w_out2, gain1, bias1, gain2, bias2, out,
    full1, full2, staged1, staged2, zbuf1, zbuf2, tiles, frames, p_in, p_out, xw, xn, qkv, mix, mid2, snd, rbuf, ret, obuf,
    z_send, z_recv, z_local, g_send1, g_recv1, g_send2, g_recv2, e1_send, e1_recv, e1_local, m_send, m_recv,
    e2_send, e2_recv, e2_local, e3_send, e3_recv, e3_local,
):
    tm, space = lax.axis_index("tm"), lax.axis_index("space")
    y, zh = lax.div(tm, 4), lax.rem(tm, 4)
    x, zl, c = lax.div(space, 4), lax.rem(lax.div(space, 2), 2), lax.rem(space, 2)
    place = (y, zh, x, zl, c)
    sibling = device(y, zh, x, zl, 1 - c)
    video_t = lax.rem(zh - y + 4, 4)
    is_self = video_t == x
    pending = []

    barrier = pltpu.get_barrier_semaphore()

    def greet(target):
        pl.semaphore_signal(barrier, inc=1, device_id=target, device_id_type=MESH)

    greet(sibling)
    for step in range(1, 8):
        greet(device(y, zh, lax.rem(x + step // 2, 4), lax.rem(zl + step % 2, 2), c))

    def greet_times(n, carry):
        other = lax.rem(tm + n, 16)
        greet((other, space))
        return carry

    lax.fori_loop(1, 16, greet_times, 0)

    def greet_sources(n, carry):
        other = lax.rem(tm + lax.div(n, 2), 16)
        zl_other = lax.rem(zl + lax.rem(n, 2), 2)

        @pl.when(jnp.logical_not(is_self & (n == 0)))
        def _():
            greet((other, video_t * 4 + zl_other * 2 + c))

        return carry

    lax.fori_loop(0, 32, greet_sources, 0)
    greet(device(y, lax.rem(zh + 2 * zl + 3, 4), x, 1 - zl, c))
    stage_shard(place, w_qkv1, w_out1, staged1)
    pl.semaphore_wait(barrier, 56 - jnp.where(is_self, 1, 0))

    g1 = gather_steps(
        place, (96, 80, False), staged1, zbuf1, full1, z_send.at[0], z_recv.at[0], z_local.at[0],
        g_send1, g_recv1, pending,
    )
    g2 = gather_steps(
        place, (96, 80, False), staged2, zbuf2, full2, z_send.at[1], z_recv.at[1], z_local.at[1],
        g_send2, g_recv2, pending,
    )
    advance(g1)

    own_tile = pltpu.make_async_copy(tokens.at[zl * 4 + x], tiles.at[space], e1_local)
    own_tile.start()
    def send_tiles(steps):
        for step in steps:
            xo, zo = lax.rem(x + step // 2, 4), lax.rem(zl + step % 2, 2)
            made = pltpu.make_async_remote_copy(
                src_ref=tokens.at[zo * 4 + xo],
                dst_ref=tiles.at[space],
                send_sem=e1_send.at[step - 1],
                recv_sem=e1_recv.at[space],
                device_id=device(y, zh, xo, zo, c),
                device_id_type=MESH,
            )
            made.start()
            pending.append(made.wait_send)

    send_tiles((2, 6, 4))
    stage_shard(place, w_qkv2, w_out2, staged2)
    frames[...] = jnp.zeros_like(frames)
    shift_r, shift_c = shifts[x, 0], shifts[x, 1]

    row = iota((ROWS, 1), 0)
    wc = div(row, WIN)
    spot = row - wc * WIN
    pr = div(spot, 14)
    pc = spot - 14 * pr
    r = wrap(14 * c + pr + shift_r, 28)
    col = wrap(14 * wc + pc + shift_c, 28)
    tile = 4 * div(r, 7) + div(col, 7)
    slot = jnp.zeros_like(tile)
    for s in range(16):
        slot = jnp.where(tile == slots[s], s, slot)
    index = slot * 64 + mod(r, 7) * 7 + mod(col, 7)
    p_in[...] = one_hot(jnp.where(spot < 196, index, -1), 1024)

    advance(g1)
    send_tiles((1, 3, 7, 5))
    advance(g2)

    row = iota((512, 1), 0)
    slot8 = div(row, 64)
    p = mod(row, 16)
    j = POS * mod(div(row, 16), 4) + p
    tile = jnp.zeros_like(row)
    for n in range(8):
        tile = jnp.where(slot8 == n, slots[4 * (n // 2) + 2 * (n % 2) + c], tile)
    jr = div(j, 7)
    r = 7 * div(tile, 4) + jr
    col = 7 * mod(tile, 4) + (j - 7 * jr)
    sr = wrap(r + 28 - shift_r, 28)
    sc = wrap(col + 28 - shift_c, 28)
    wr, wc = div(sr, 14), div(sc, 14)
    index = wr * ROWS + wc * WIN + (sr - 14 * wr) * 14 + (sc - 14 * wc)
    p_out[...] = one_hot(jnp.where((p < POS) & (j < 49), index, -1), 2 * ROWS)

    advance(g1)

    own_tile.wait()

    def tile_copy(s, n):
        return pltpu.make_async_remote_copy(
            src_ref=tiles.at[s],
            dst_ref=tiles.at[s],
            send_sem=e1_send.at[7 + n],
            recv_sem=e1_recv.at[s],
            device_id=sibling,
            device_id_type=MESH,
        )

    for n, step in enumerate((0, 2, 6, 1, 3, 7, 4, 5)):
        xo, zo = lax.rem(x + step // 2, 4), lax.rem(zl + step % 2, 2)
        s = xo * 4 + zo * 2 + c
        made = tile_copy(s, n)
        if step:
            made.wait_recv()
        made.start()
        pending.append(made.wait_send)
    advance(g1)
    advance(g1)
    for step in range(8):
        s = 4 * (step // 2) + 2 * (step % 2) + 1 - c
        tile_copy(s, 0).wait_recv()

    def widen(s, carry):
        frames[s, :49, :] = tiles[s]
        return carry

    lax.fori_loop(0, 16, widen, 0)
    for first, width in PARTS:
        columns = slice(first, first + width)
        cells = frames[:, :, columns].reshape(1024, width)
        xw[:, columns] = matmul(p_in[...], cells).astype(BF16)
        advance(g1)

    def in_window(rows):
        return rows - jnp.where(rows >= WIN, WIN, 0) < 196

    normalize(xw, xn, gain1, bias1, in_window)
    for n in range(5):
        advance(g1)
    advance(g2)
    advance(g1)
    for kind in range(3):
        project(xn, full1, qkv, kind)
        if kind:
            advance(g2)

    def regions(shape, axis, column):
        at = iota(shape, axis)
        down = div(at, 14)
        across = at - 14 * down
        kind = 2 * jnp.where(14 * c + down >= 28 - shift_r, 1, 0)
        kind = kind + jnp.where(14 * column + across >= 28 - shift_c, 1, 0)
        return jnp.where(at < 196, kind, -1)

    for column in range(2):
        allowed = regions((WIN, 1), 0, column) == regions((1, WIN), 1, column)
        attend(qkv, mix, pl.ds(column * WIN, WIN), allowed)
        advance(g2)

    def swap(n, core):
        first, width = PARTS[n]
        piece = mid2.at[core, :, pl.ds(first, width)]
        return pltpu.make_async_remote_copy(
            src_ref=piece,
            dst_ref=piece,
            send_sem=m_send.at[n],
            recv_sem=m_recv.at[n],
            device_id=sibling,
            device_id_type=MESH,
        )

    for n, (first, width) in enumerate(PARTS):
        mid2[c, :, first : first + width] = out_project(mix, full1, xw, slice(first, first + width))
        swap(n, c).start()
        pending.append(swap(n, c).wait_send)
        advance(g2)

    time = 2 * tm + zl

    def row_copy(n, part):
        dx, dz, dq = lax.div(n, 8), lax.rem(lax.div(n, 4), 2), lax.rem(n, 4)
        xo, zo, q = lax.rem(x + dx, 4), lax.rem(zl + dz, 2), lax.rem(y + dq, 4)
        columns = pl.ds(*PARTS[part])
        return pltpu.make_async_remote_copy(
            src_ref=snd.at[(xo * 2 + zo) * 4 + q, :, columns],
            dst_ref=rbuf.at[time, :, columns],
            send_sem=e2_send.at[part, n],
            recv_sem=e2_recv.at[part, time],
            device_id=device(q, lax.rem(q + x, 4), xo, zo, c),
            device_id_type=MESH,
        )

    for part, (first, width) in enumerate(PARTS):
        columns = slice(first, first + width)
        swap(part, 1 - c).wait_recv()
        cells = mid2[:, :, columns].reshape(2 * ROWS, width)
        snd[:, :, columns] = matmul(p_out[...], cells).astype(BF16).reshape(32, 16, width)

        def start_rows(n, carry):
            @pl.when(jnp.logical_not(is_self & (n == 0)))
            def _():
                row_copy(n, part).start()

            return carry

        lax.fori_loop(0, 32, start_rows, 0)

    @pl.when(is_self)
    def _():
        own_rows = pltpu.make_async_copy(snd.at[(x * 2 + zl) * 4 + y], rbuf.at[time], e2_local)
        own_rows.start()
        own_rows.wait()

    for n in range(8):
        advance(g2)

    row = iota((TROWS, 1), 0)
    at = div(row, 32)
    by_position = one_hot((row - 32 * at) * 16 + at, 512)

    for part, (first, width) in enumerate(PARTS):
        columns = slice(first, first + width)

        def wait_rows(n, carry):
            @pl.when(jnp.logical_not(is_self & (n == time)))
            def _():
                piece = rbuf.at[n, :, pl.ds(first, width)]
                pltpu.make_async_remote_copy(
                    src_ref=piece,
                    dst_ref=piece,
                    send_sem=e2_send.at[part, 0],
                    recv_sem=e2_recv.at[part, n],
                    device_id=sibling,
                    device_id_type=MESH,
                ).wait_recv()

            return carry

        lax.fori_loop(0, 32, wait_rows, 0)
        cells = rbuf[:, :, columns].reshape(512, width)
        xw[:, columns] = matmul(by_position, cells).astype(BF16)

    normalize(xw, xn, gain2, bias2, lambda rows: div(rows, 32) + POS * y < 49)
    advance(g2)
    for kind in range(3):
        project(xn, full2, qkv, kind)

    for first, count in ((0, 128), (128, 128), (256, 128), (384, 32)):
        left, right = iota((count, 1), 0), iota((1, count), 1)
        attend(qkv, mix, pl.ds(first, count), div(left, 32) == div(right, 32))

    row = iota((512, 1), 0)
    at = div(row, 16)
    p = row - 16 * at
    by_time = one_hot(jnp.where(p < POS, p * 32 + at, -1), TROWS)

    def back_copy(n, part):
        other = lax.rem(tm + n, 16)
        columns = pl.ds(*PARTS[part])
        return pltpu.make_async_remote_copy(
            src_ref=ret.at[pl.ds(2 * other, 2), :, columns],
            dst_ref=obuf.at[tm, :, :, columns],
            send_sem=e3_send.at[part, n],
            recv_sem=e3_recv.at[part, tm],
            device_id=(other, space),
            device_id_type=MESH,
        )

    for part, (first, width) in enumerate(PARTS):
        columns = slice(first, first + width)
        encoded = out_project(mix, full2, xw, columns)
        ret[:, :, columns] = matmul(by_time, encoded).astype(BF16).reshape(32, 16, width)

        def start_back(n, carry):
            back_copy(n, part).start()
            return carry

        lax.fori_loop(1, 16, start_back, 0)
    own_back = pltpu.make_async_copy(ret.at[pl.ds(2 * tm, 2)], obuf.at[tm], e3_local)
    own_back.start()
    own_back.wait()

    row = iota((64, 1), 0)
    q = div(row, POS)
    join = one_hot(jnp.where(row < 49, q * 16 + row - POS * q, -1), 64)
    for part, (first, width) in enumerate(PARTS):
        columns = slice(first, first + width)

        def wait_back(n, carry):
            piece = obuf.at[lax.rem(tm + n, 16), :, :, pl.ds(first, width)]
            pltpu.make_async_remote_copy(
                src_ref=piece,
                dst_ref=piece,
                send_sem=e3_send.at[part, 0],
                recv_sem=e3_recv.at[part, lax.rem(tm + n, 16)],
                device_id=sibling,
                device_id_type=MESH,
            ).wait_recv()
            return carry

        lax.fori_loop(1, 16, wait_back, 0)
        for t in range(2):
            for v in range(4):
                parts = [obuf[4 * n + (n + v) % 4, t, :, columns] for n in range(4)]
                whole = matmul(join, jnp.concatenate(parts, axis=0)).astype(BF16)
                out[t, v, :, columns] = whole[:49]

    for finish in pending:
        finish()

    for part in range(len(PARTS)):
        def finish_rows(n, carry):
            @pl.when(jnp.logical_not(is_self & (n == 0)))
            def _():
                row_copy(n, part).wait_send()

            return carry

        lax.fori_loop(0, 32, finish_rows, 0)

        def finish_back(n, carry):
            back_copy(n, part).wait_send()
            return carry

        lax.fori_loop(1, 16, finish_back, 0)


def body(
    tokens, tile_of_slot, shifts, norm_gain_space, norm_bias_space, w_qkv_space, w_out_space,
    norm_gain_time, norm_bias_time, w_qkv_time, w_out_time,
):
    smem = pl.BlockSpec(memory_space=pltpu.SMEM)
    vmem = pl.BlockSpec(memory_space=pltpu.VMEM)
    anywhere = pl.BlockSpec(memory_space=pl.ANY)
    dma = pltpu.SemaphoreType.DMA
    encoded = pl.pallas_call(
        kernel,
        out_shape=jax.ShapeDtypeStruct((2, 4, 49, D), BF16),
        in_specs=[smem, smem, anywhere] + [vmem] * 8,
        out_specs=vmem,
        scratch_shapes=[
            pltpu.VMEM((4, D, EP), BF16),
            pltpu.VMEM((4, D, EP), BF16),
            pltpu.VMEM((88, EP), BF16),
            pltpu.VMEM((88, EP), BF16),
            pltpu.VMEM((2, 88, EP), BF16),
            pltpu.VMEM((2, 88, EP), BF16),
            pltpu.VMEM((16, 49, D), BF16),
            pltpu.VMEM((16, 64, D), BF16),
            pltpu.VMEM((ROWS, 1024), BF16),
            pltpu.VMEM((512, 2 * ROWS), BF16),
            pltpu.VMEM((ROWS, D), BF16),
            pltpu.VMEM((ROWS, D), BF16),
            pltpu.VMEM((3, ROWS, EP), BF16),
            pltpu.VMEM((ROWS, EP), BF16),
            pltpu.VMEM((2, ROWS, D), BF16),
            pltpu.VMEM((32, 16, D), BF16),
            pltpu.VMEM((32, 16, D), BF16),
            pltpu.VMEM((32, 16, D), BF16),
            pltpu.VMEM((16, 2, 16, D), BF16),
            dma((2, 3)), dma((2, 2)), dma((2,)), dma((COPIES[0],)), dma((COPIES[0],)), dma((COPIES[1],)), dma((COPIES[1],)),
            dma((15,)), dma((16,)), dma, dma((2,)), dma((2,)),
            dma((2, 32)), dma((2, 32)), dma, dma((2, 16)), dma((2, 16)), dma,
        ],
        compiler_params=pltpu.CompilerParams(
            collective_id=0, has_side_effects=True, vmem_limit_bytes=60 * 1024 * 1024
        ),
        cost_estimate=pl.CostEstimate(flops=12_000_000_000, bytes_accessed=40_000_000, transcendentals=2_000_000),
    )(
        tile_of_slot, shifts, tokens.reshape(8, 49, D), w_qkv_space, w_out_space, w_qkv_time, w_out_time,
        norm_gain_space, norm_bias_space, norm_gain_time, norm_bias_time,
    )
    return encoded.reshape(tokens.shape)


def solution(mesh):
    placed = (
        P("tm", "space", None, None, None), P(), P(), P(), P(), P("tm", None), P(None, "tm"),
        P(), P(), P("tm", None), P(None, "tm"),
    )
    return jax.shard_map(
        body,
        mesh=mesh,
        in_specs=placed,
        out_specs=P("tm", "space", None, None, None),
        check_vma=False,
    )
```

```python
import functools

import jax
import jax.numpy as jnp
from jax import lax
from jax.experimental import pallas as pl
from jax.experimental.pallas import tpu as pltpu
from jax.sharding import PartitionSpec as P

HEADS = 12
HEAD_DIM = 88
D = 1408
E = 1056
EP = 1152
WIN = 208
ROWS = 2 * WIN
TROWS = 512
EPSILON = 1e-06
SCALE = HEAD_DIM ** (-0.5)
MESH = pl.DeviceIdType.MESH
F32 = jnp.float32
BF16 = jnp.bfloat16
COPIES = (72, 72)
PARTS = ((0, 768), (768, 640))


def div(values, by):
    return lax.shift_right_logical(values * (-(-65536 // by)), 16)


def mod(values, by):
    return values - by * div(values, by)


def wrap(values, size):
    return values - jnp.where(values >= size, size, 0)


def iota(shape, axis):
    return lax.broadcasted_iota(jnp.int32, shape, axis)


def one_hot(index, columns):
    hit = index == iota((index.shape[0], columns), 1)
    return jnp.where(hit, F32(1.0), F32(0.0)).astype(BF16)


def matmul(left, right):
    return jnp.dot(left, right, preferred_element_type=F32)


def matmul_nt(left, right):
    return lax.dot_general(left, right, (((1,), (1,)), ((), ())), preferred_element_type=F32)


def normalize(source, target, gain_ref, bias_ref, count, valid):
    def one(n, carry):
        rows = pl.ds(pl.multiple_of(n * 32, 32), 32)
        widened = source[rows, :].astype(F32)
        average = jnp.mean(widened, axis=-1, keepdims=True)
        centered = widened - average
        variance = jnp.mean(centered * centered, axis=-1, keepdims=True)
        normed = centered * lax.rsqrt(variance + EPSILON) * gain_ref[...] + bias_ref[...]
        keep = valid(n * 32 + iota((32, 1), 0))
        target[rows, :] = jnp.where(keep, normed, F32(0.0)).astype(BF16)
        return carry

    lax.fori_loop(0, count // 32, one, 0)


def project(normed, full, qkv, kind, count):
    qkv[kind, :count, :] = matmul(normed[:count, :], full[kind]).astype(BF16)


def attend(qkv, mix, rows, allowed):
    count = allowed.shape[0]
    partial = None
    for head in range(HEADS):
        low = HEAD_DIM * head
        first = low // 128 * 128
        last = -(-(low + HEAD_DIM) // 128) * 128
        lane = first + iota((count, last - first), 1)
        own = (lane >= low) & (lane < low + HEAD_DIM)
        zero = jnp.zeros((count, last - first), BF16)
        query = qkv[0, rows, first:last]
        keys = jnp.where(own, qkv[1, rows, first:last], zero)
        values = jnp.where(own, qkv[2, rows, first:last], zero)
        weights = jnp.where(allowed, jnp.exp(matmul_nt(query, keys) * SCALE), F32(0.0))
        total = jnp.sum(weights, axis=-1, keepdims=True)
        shares = (weights * (1.0 / total)).astype(BF16)
        mixed = matmul(shares, values)
        pieces = [mixed[:, n : n + 128] for n in range(0, last - first, 128)]
        if partial is not None:
            pieces[0] = pieces[0] + partial
        partial = None
        if head < HEADS - 1 and (low + HEAD_DIM) % 128:
            partial = pieces.pop()
        for n, piece in enumerate(pieces):
            mix[rows, first + 128 * n : first + 128 * n + 128] = piece.astype(BF16)


def out_project(mix, full, residual, columns, count):
    product = matmul_nt(mix[:count, :], full[3, columns, :])
    return (residual[:count, columns].astype(F32) + product).astype(BF16)


def stage_shard(place, w_qkv, w_out, staged):
    x = place[2]
    staged[...] = jnp.zeros_like(staged)
    for kind in range(3):
        @pl.when(x == kind)
        def _():
            staged[:, :E] = w_qkv[:, E * kind : E * kind + E]

    @pl.when(x == 3)
    def _():
        staged[:, :E] = w_out[...]


def gather_steps(place, sizes, staged, zbuf, full, z_send, z_recv, z_local, send_sem, recv_sem, pending):
    y, zh, x, zl, c = place
    dev = device
    core_of = lax.div(zh, 2)
    is_sender = core_of == c
    mine = lax.rem(zh, 2)

    def z_copy(step):
        return pltpu.make_async_remote_copy(
            src_ref=staged,
            dst_ref=zbuf.at[mine],
            send_sem=z_send.at[step - 1],
            recv_sem=z_recv.at[mine],
            device_id=dev(y, lax.rem(zh + step, 4), x, zl, c),
            device_id_type=MESH,
        )

    def z_own():
        return pltpu.make_async_copy(staged, zbuf.at[mine], z_local)

    @pl.when(is_sender)
    def _():
        for step in (1, 3, 2):
            z_copy(step).start()
        z_own().start()

    def z_finish():
        @pl.when(is_sender)
        def _():
            for step in (1, 3, 2):
                z_copy(step).wait_send()

    pending.append(z_finish)
    yield

    for k in range(2):
        @pl.when(zh != 2 * c + k)
        def _():
            pltpu.make_async_remote_copy(
                src_ref=staged,
                dst_ref=zbuf.at[k],
                send_sem=z_send.at[0],
                recv_sem=z_recv.at[k],
                device_id=dev(y, zh, x, zl, 1 - c),
                device_id_type=MESH,
            ).wait_recv()

    @pl.when(is_sender)
    def _():
        z_own().wait()

    def region(kind, row, core, low, count):
        start = pl.multiple_of(352 * lax.rem(y + row + 4, 4) + 176 * core + low, 16)
        return full.at[lax.rem(x + kind + 4, 4), pl.ds(start, count), :]

    rows_a, rows_b, split_z = sizes
    low_a = (176 - rows_a) * zl if split_z else 0
    low_b = rows_a - (rows_a - 48) * zl if split_z else rows_a
    base = pl.multiple_of(352 * y + 176 * c, 16)
    both = jnp.concatenate([zbuf[0].astype(F32), zbuf[1].astype(F32)], axis=0)
    full[x, pl.ds(base, 176), :] = both.astype(BF16)

    xp, xm = dev(y, zh, lax.rem(x + 1, 4), zl, c), dev(y, zh, lax.rem(x + 3, 4), zl, c)
    yp, ym = dev(lax.rem(y + 1, 4), zh, x, zl, c), dev(lax.rem(y + 3, 4), zh, x, zl, c)
    sibling = dev(y, zh, x, zl, 1 - c)
    counter = [0]

    def copy(k, piece, target):
        return pltpu.make_async_remote_copy(
            src_ref=piece,
            dst_ref=piece,
            send_sem=send_sem.at[k],
            recv_sem=recv_sem.at[k],
            device_id=target,
            device_id_type=MESH,
        )

    def send(piece, target):
        k = counter[0]
        counter[0] += 1
        made = copy(k, piece, target)
        made.start()
        pending.append(made.wait_send)
        return k

    def recv(k, piece):
        copy(k, piece, sibling).wait_recv()

    def part_a(kind, row, low=0, count=rows_a, core=c):
        return region(kind, row, core, low_a + low, count)

    def part_b(kind, row, low=0, count=rows_b, core=c):
        return region(kind, row, core, low_b + low, count)

    def part_z(kind, row, parity, low=0, count=48, core=c):
        return region(kind, row, core, 128 * parity + low, count)

    arriving = []
    half_a = 16 * ((rows_a // 16 + 1) // 2)
    half_b = 16 * ((rows_b // 16 + 1) // 2)

    inner = dev(y, zh, x, 1 - zl, c)
    outer = dev(y, lax.rem(zh + 2 * zl + 3, 4), x, 1 - zl, c)
    crossing = []

    def share(part, kind, row):
        arriving.append((send(part(kind, row), sibling), part(kind, row, core=1 - c)))
        if not split_z or part is not part_a:
            return
        if kind == 0 and row == 0:
            k = send(part_z(0, 0, 1 - zl), sibling)
            arriving.append((k, part_z(0, 0, 1 - zl, core=1 - c)))
        else:
            k_out = send(part_z(kind, row, zl, 0, 32), outer)
            k_in = send(part_z(kind, row, zl, 32, 16), inner)
            crossing.append((kind, row, k_out, k_in))

    def crossed(count):
        for kind, row, k_out, k_in in crossing[:count]:
            recv(k_out, part_z(kind, row, 1 - zl, 0, 32))
            recv(k_in, part_z(kind, row, 1 - zl, 32, 16))
            k = send(part_z(kind, row, 1 - zl), sibling)
            arriving.append((k, part_z(kind, row, 1 - zl, core=1 - c)))
        del crossing[:count]

    class Ring:
        def __init__(self, part, along_x, at, plus, minus, halves):
            self.part, self.along_x, self.at = part, along_x, at
            self.plus, self.minus, self.halves = plus, minus, halves
            own = self.piece(0)
            self.k_plus = send(own, plus)
            self.k_minus = send(own, minus)

        def spot(self, step):
            return (step, self.at) if self.along_x else (self.at, step)

        def piece(self, step, *cut):
            return self.part(*self.spot(step), *cut)

        def near(self):
            low, high = self.halves
            recv(self.k_plus, self.piece(-1))
            self.f_plus = send(self.piece(-1, 0, low), self.plus)
            recv(self.k_minus, self.piece(1))
            self.f_minus = send(self.piece(1, low, high), self.minus)

        def far(self):
            low, high = self.halves
            recv(self.f_plus, self.piece(2, 0, low))
            recv(self.f_minus, self.piece(2, low, high))

    def ring_a1():
        return Ring(part_a, True, 0, xp, xm, (half_a, rows_a - half_a))

    def ring_b1():
        return Ring(part_b, False, 0, yp, ym, (half_b, rows_b - half_b))

    def ring_a2(kind):
        return Ring(part_a, False, kind, yp, ym, (half_a, rows_a - half_a))

    def ring_b2(row):
        return Ring(part_b, True, row, xp, xm, (half_b, rows_b - half_b))

    a1, b1 = ring_a1(), ring_b1()
    seconds = [ring_a2(0), ring_b2(0)]
    share(part_a, 0, 0)
    share(part_b, 0, 0)
    yield
    a1.near()
    b1.near()
    for step in (-1, 1):
        seconds += [ring_a2(step), ring_b2(step)]
    for step in (-1, 1):
        share(part_a, step, 0)
        share(part_b, 0, step)
    yield
    a1.far()
    b1.far()
    seconds += [ring_a2(2), ring_b2(2)]
    share(part_a, 2, 0)
    share(part_b, 0, 2)
    yield
    for n in range(0, 8, 2):
        for ring in seconds[n : n + 2]:
            ring.near()
            for step in (-1, 1):
                share(ring.part, *ring.spot(step))
        yield
    for n in range(0, 8, 2):
        for ring in seconds[n : n + 2]:
            ring.far()
            share(ring.part, *ring.spot(2))
        if n < 6:
            yield
    yield
    crossed(len(crossing))
    for k, piece in arriving:
        recv(k, piece)
    assert counter[0] == send_sem.shape[0], counter
    yield


def device(y, zh, x, zl, c):
    return (y * 4 + zh, x * 4 + zl * 2 + c)


def advance(steps):
    next(steps, None)


def kernel(
    slots, shifts, tokens, w_qkv1, w_out1, w_qkv2, w_out2, gain1, bias1, gain2, bias2, out,
    full1, full2, staged1, staged2, zbuf1, zbuf2, tiles, frames, p_in, p_out, xw, xn, qkv, mix, mid2, snd, rbuf, ret, obuf,
    snd_one, rbuf_one, ret_one, obuf_one, wide, by_time,
    z_send, z_recv, z_local, g_send1, g_recv1, g_send2, g_recv2, e1_send, e1_recv, e1_local, m_send, m_recv,
    e2_send, e2_recv, e2_local, e3_send, e3_recv, e3_local,
):
    tm, space = lax.axis_index("tm"), lax.axis_index("space")
    y, zh = lax.div(tm, 4), lax.rem(tm, 4)
    x, zl, c = lax.div(space, 4), lax.rem(lax.div(space, 2), 2), lax.rem(space, 2)
    place = (y, zh, x, zl, c)
    sibling = device(y, zh, x, zl, 1 - c)
    video_t = lax.rem(zh + y, 4)
    is_self = video_t == x
    quarter = lax.rem(zh + 2 * zl + c, 4)
    single = quarter == 3
    pending = []

    barrier = pltpu.get_barrier_semaphore()

    def greet(target):
        pl.semaphore_signal(barrier, inc=1, device_id=target, device_id_type=MESH)

    greet(sibling)
    for step in range(1, 8):
        greet(device(y, zh, lax.rem(x + step // 2, 4), lax.rem(zl + step % 2, 2), c))

    def greet_times(n, carry):
        other = lax.rem(tm + n, 16)
        greet((other, space))
        return carry

    lax.fori_loop(1, 16, greet_times, 0)

    def greet_sources(n, carry):
        other = lax.rem(tm + lax.div(n, 2), 16)
        zl_other = lax.rem(zl + lax.rem(n, 2), 2)

        @pl.when(jnp.logical_not(is_self & (n == 0)))
        def _():
            greet((other, video_t * 4 + zl_other * 2 + c))

        return carry

    lax.fori_loop(0, 32, greet_sources, 0)
    greet(device(y, lax.rem(zh + 2 * zl + 3, 4), x, 1 - zl, c))
    stage_shard(place, w_qkv1, w_out1, staged1)
    pl.semaphore_wait(barrier, 56 - jnp.where(is_self, 1, 0))

    g1 = gather_steps(
        place, (96, 80, False), staged1, zbuf1, full1, z_send.at[0], z_recv.at[0], z_local.at[0],
        g_send1, g_recv1, pending,
    )
    g2 = gather_steps(
        place, (96, 80, False), staged2, zbuf2, full2, z_send.at[1], z_recv.at[1], z_local.at[1],
        g_send2, g_recv2, pending,
    )
    advance(g1)

    own_tile = pltpu.make_async_copy(tokens.at[zl * 4 + x], tiles.at[space], e1_local)
    own_tile.start()
    def send_tiles(steps):
        for step in steps:
            xo, zo = lax.rem(x + step // 2, 4), lax.rem(zl + step % 2, 2)
            made = pltpu.make_async_remote_copy(
                src_ref=tokens.at[zo * 4 + xo],
                dst_ref=tiles.at[space],
                send_sem=e1_send.at[step - 1],
                recv_sem=e1_recv.at[space],
                device_id=device(y, zh, xo, zo, c),
                device_id_type=MESH,
            )
            made.start()
            pending.append(made.wait_send)

    send_tiles((2, 6, 4))
    stage_shard(place, w_qkv2, w_out2, staged2)
    wide[...] = jnp.zeros_like(wide)
    frames[...] = jnp.zeros_like(frames)
    shift_r, shift_c = shifts[0, x], shifts[1, x]

    row = iota((ROWS, 1), 0)
    wc = div(row, WIN)
    spot = row - wc * WIN
    pr = div(spot, 14)
    pc = spot - 14 * pr
    r = wrap(14 * c + pr + shift_r, 28)
    col = wrap(14 * wc + pc + shift_c, 28)
    tile = 4 * div(r, 7) + div(col, 7)
    slot = jnp.zeros_like(tile)
    for s in range(16):
        slot = jnp.where(tile == slots[s], s, slot)
    index = slot * 64 + mod(r, 7) * 7 + mod(col, 7)
    p_in[...] = one_hot(jnp.where(spot < 196, index, -1), 1024)

    advance(g1)
    send_tiles((1, 3, 7, 5))
    advance(g2)

    row = iota((400, 1), 0)
    last = row >= 384
    slot8 = jnp.where(last, row - 384, div(row, 48))
    j = jnp.where(last, 48, row - 48 * slot8)
    tile = jnp.zeros_like(row)
    for n in range(8):
        tile = jnp.where(slot8 == n, slots[4 * (n // 2) + 2 * (n % 2) + c], tile)
    jr = div(j, 7)
    r = 7 * div(tile, 4) + jr
    col = 7 * mod(tile, 4) + (j - 7 * jr)
    sr = wrap(r + 28 - shift_r, 28)
    sc = wrap(col + 28 - shift_c, 28)
    wr, wc = div(sr, 14), div(sc, 14)
    index = wr * ROWS + wc * WIN + (sr - 14 * wr) * 14 + (sc - 14 * wc)
    p_out[...] = one_hot(jnp.where(slot8 < 8, index, -1), 2 * ROWS)

    advance(g1)

    own_tile.wait()

    def tile_copy(s, n):
        return pltpu.make_async_remote_copy(
            src_ref=tiles.at[s],
            dst_ref=tiles.at[s],
            send_sem=e1_send.at[7 + n],
            recv_sem=e1_recv.at[s],
            device_id=sibling,
            device_id_type=MESH,
        )

    for n, step in enumerate((0, 2, 6, 1, 3, 7, 4, 5)):
        xo, zo = lax.rem(x + step // 2, 4), lax.rem(zl + step % 2, 2)
        s = xo * 4 + zo * 2 + c
        made = tile_copy(s, n)
        if step:
            made.wait_recv()
        made.start()
        pending.append(made.wait_send)
    advance(g1)
    advance(g1)
    for step in range(8):
        s = 4 * (step // 2) + 2 * (step % 2) + 1 - c
        tile_copy(s, 0).wait_recv()

    def widen(s, carry):
        frames[s, :49, :] = tiles[s]
        return carry

    lax.fori_loop(0, 16, widen, 0)
    for first, width in PARTS:
        columns = slice(first, first + width)
        cells = frames[:, :, columns].reshape(1024, width)
        xw[:ROWS, columns] = matmul(p_in[...], cells).astype(BF16)
        advance(g1)

    def in_window(rows):
        return rows - jnp.where(rows >= WIN, WIN, 0) < 196

    normalize(xw, xn, gain1, bias1, ROWS, in_window)
    for n in range(5):
        advance(g1)
    advance(g2)
    advance(g1)
    for kind in range(3):
        project(xn, full1, qkv, kind, ROWS)
        if kind:
            advance(g2)

    def regions(shape, axis, column):
        at = iota(shape, axis)
        down = div(at, 14)
        across = at - 14 * down
        kind = 2 * jnp.where(14 * c + down >= 28 - shift_r, 1, 0)
        kind = kind + jnp.where(14 * column + across >= 28 - shift_c, 1, 0)
        return jnp.where(at < 196, kind, -1)

    for column in range(2):
        allowed = regions((WIN, 1), 0, column) == regions((1, WIN), 1, column)
        attend(qkv, mix, pl.ds(column * WIN, WIN), allowed)
        advance(g2)

    def swap(n, core):
        first, width = PARTS[n]
        piece = mid2.at[core, :, pl.ds(first, width)]
        return pltpu.make_async_remote_copy(
            src_ref=piece,
            dst_ref=piece,
            send_sem=m_send.at[n],
            recv_sem=m_recv.at[n],
            device_id=sibling,
            device_id_type=MESH,
        )

    for n, (first, width) in enumerate(PARTS):
        mid2[c, :, first : first + width] = out_project(mix, full1, xw, slice(first, first + width), ROWS)
        swap(n, c).start()
        pending.append(swap(n, c).wait_send)
        advance(g2)

    time = 2 * tm + zl

    def row_target(n):
        dx, dz, dh = lax.div(n, 8), lax.rem(lax.div(n, 4), 2), lax.rem(n, 4)
        xo, zo, ho = lax.rem(x + dx, 4), lax.rem(zl + dz, 2), lax.rem(zh + dh, 4)
        target = device(lax.rem(x - ho + 4, 4), ho, xo, zo, c)
        return xo * 2 + zo, lax.rem(ho + 2 * zo + c, 4), target

    def row_copy(n, part):
        s, q, target = row_target(n)
        columns = pl.ds(*PARTS[part])
        return pltpu.make_async_remote_copy(
            src_ref=snd.at[s * 3 + q, :, columns],
            dst_ref=rbuf.at[time, :, columns],
            send_sem=e2_send.at[part, n],
            recv_sem=e2_recv.at[part, time],
            device_id=target,
            device_id_type=MESH,
        )

    def one_copy(n):
        s, q, target = row_target(n)
        return pltpu.make_async_remote_copy(
            src_ref=snd_one.at[s],
            dst_ref=rbuf_one.at[time],
            send_sem=e2_send.at[1, n],
            recv_sem=e2_recv.at[1, time],
            device_id=target,
            device_id_type=MESH,
        )

    def each_row(n, part, do):
        away = jnp.logical_not(is_self & (n == 0))
        q = row_target(n)[1]

        @pl.when(away & (q < 3))
        def _():
            do(row_copy(n, part))

        if part:
            @pl.when(away & (q == 3))
            def _():
                do(one_copy(n))

    for part, (first, width) in enumerate(PARTS):
        columns = slice(first, first + width)
        swap(part, 1 - c).wait_recv()
        cells = mid2[:, :, columns].reshape(2 * ROWS, width)
        moved = matmul(p_out[...], cells)
        snd[:, :, columns] = moved[:384].astype(BF16).reshape(24, 16, width)
        for n in range(width // 128):
            wide[:8, first // 128 + n, :] = moved[384:392, 128 * n : 128 * n + 128]
        if part:
            snd_one[...] = wide[:8].astype(BF16)

        def start_rows(n, carry):
            each_row(n, part, lambda made: made.start())
            return carry

        lax.fori_loop(0, 32, start_rows, 0)

    @pl.when(is_self & jnp.logical_not(single))
    def _():
        own_rows = pltpu.make_async_copy(snd.at[(x * 2 + zl) * 3 + quarter], rbuf.at[time], e2_local)
        own_rows.start()
        own_rows.wait()

    @pl.when(is_self & single)
    def _():
        own_rows = pltpu.make_async_copy(snd_one.at[x * 2 + zl], rbuf_one.at[time], e2_local)
        own_rows.start()
        own_rows.wait()

    for n in range(8):
        advance(g2)

    row = iota((TROWS, 1), 0)
    at = div(row, 32)
    by_position = one_hot((row - 32 * at) * 16 + at, TROWS)

    at = div(row, 16)
    p = row - 16 * at
    by_time[...] = one_hot(p * 32 + at, TROWS)

    def wait_landed(piece, part, n):
        pltpu.make_async_remote_copy(
            src_ref=piece,
            dst_ref=piece,
            send_sem=e2_send.at[part, 0],
            recv_sem=e2_recv.at[part, n],
            device_id=sibling,
            device_id_type=MESH,
        ).wait_recv()

    @pl.when(jnp.logical_not(single))
    def _():
        for part, (first, width) in enumerate(PARTS):
            columns = slice(first, first + width)

            def wait_rows(n, carry):
                @pl.when(jnp.logical_not(is_self & (n == time)))
                def _():
                    wait_landed(rbuf.at[n, :, pl.ds(first, width)], part, n)

                return carry

            lax.fori_loop(0, 32, wait_rows, 0)
            cells = rbuf[:, :, columns].reshape(TROWS, width)
            xw[:, columns] = matmul(by_position, cells).astype(BF16)

    @pl.when(single)
    def _():
        def wait_ones(n, carry):
            @pl.when(jnp.logical_not(is_self & (n == time)))
            def _():
                wait_landed(rbuf_one.at[n], 1, n)

            return carry

        lax.fori_loop(0, 32, wait_ones, 0)
        xw[...] = jnp.zeros_like(xw)
        wide[...] = rbuf_one[...].astype(F32)
        for n in range(11):
            xw[:32, 128 * n : 128 * n + 128] = wide[:, n, :].astype(BF16)

    normalize(xw, xn, gain2, bias2, TROWS, lambda rows: jnp.logical_not(single) | (rows < 32))
    advance(g2)
    for kind in range(3):
        project(xn, full2, qkv, kind, TROWS)

    def attend_group(n, carry):
        left, right = iota((128, 1), 0), iota((1, 128), 1)
        rows = pl.ds(pl.multiple_of(n * 128, 128), 128)
        attend(qkv, mix, rows, div(left, 32) == div(right, 32))
        return carry

    lax.fori_loop(0, 4, attend_group, 0)

    def back_copy(n, part):
        other = lax.rem(tm + n, 16)
        columns = pl.ds(*PARTS[part])
        return pltpu.make_async_remote_copy(
            src_ref=ret.at[pl.ds(2 * other, 2), :, columns],
            dst_ref=obuf.at[tm, :, :, columns],
            send_sem=e3_send.at[part, n],
            recv_sem=e3_recv.at[part, tm],
            device_id=(other, space),
            device_id_type=MESH,
        )

    def back_one(n):
        other = lax.rem(tm + n, 16)
        return pltpu.make_async_remote_copy(
            src_ref=ret_one.at[pl.ds(2 * other, 2)],
            dst_ref=obuf_one.at[tm],
            send_sem=e3_send.at[1, n],
            recv_sem=e3_recv.at[1, tm],
            device_id=(other, space),
            device_id_type=MESH,
        )

    def all_back(part, do):
        @pl.when(jnp.logical_not(single))
        def _():
            def one(n, carry):
                do(back_copy(n, part))
                return carry

            lax.fori_loop(1, 16, one, 0)

        if part:
            @pl.when(single)
            def _():
                def one(n, carry):
                    do(back_one(n))
                    return carry

                lax.fori_loop(1, 16, one, 0)

    for part, (first, width) in enumerate(PARTS):
        columns = slice(first, first + width)
        encoded = out_project(mix, full2, xw, columns, TROWS)
        ret[:, :, columns] = matmul(by_time[...], encoded).astype(BF16).reshape(32, 16, width)
        for n in range(width // 128):
            wide[:, first // 128 + n, :] = encoded[:32, 128 * n : 128 * n + 128].astype(F32)
        if part:
            ret_one[...] = wide[...].astype(BF16)
        all_back(part, lambda made: made.start())

    @pl.when(jnp.logical_not(single))
    def _():
        own_back = pltpu.make_async_copy(ret.at[pl.ds(2 * tm, 2)], obuf.at[tm], e3_local)
        own_back.start()
        own_back.wait()

    @pl.when(single)
    def _():
        own_back = pltpu.make_async_copy(ret_one.at[pl.ds(2 * tm, 2)], obuf_one.at[tm], e3_local)
        own_back.start()
        own_back.wait()

    for finish in pending:
        finish()

    for part in range(len(PARTS)):
        def finish_rows(n, carry):
            each_row(n, part, lambda made: made.wait_send())
            return carry

        lax.fori_loop(0, 32, finish_rows, 0)

    def wait_back(piece, part, n):
        pltpu.make_async_remote_copy(
            src_ref=piece,
            dst_ref=piece,
            send_sem=e3_send.at[part, 0],
            recv_sem=e3_recv.at[part, n],
            device_id=sibling,
            device_id_type=MESH,
        ).wait_recv()

    for part, (first, width) in enumerate(PARTS):
        columns = slice(first, first + width)

        def land(n, carry):
            q = lax.rem(lax.rem(n, 4) + 2 * zl + c, 4)

            @pl.when((n != tm) & (q < 3))
            def _():
                wait_back(obuf.at[n, :, :, pl.ds(first, width)], part, n)

            if part:
                @pl.when((n != tm) & (q == 3))
                def _():
                    wait_back(obuf_one.at[n], part, n)

            return carry

        lax.fori_loop(0, 16, land, 0)
        for q in range(3):
            for v in range(4):
                ho = lax.rem(q + 8 - 2 * zl - c, 4)
                n = lax.rem(v - ho + 4, 4) * 4 + ho
                for t in range(2):
                    out[t, v, 16 * q : 16 * q + 16, columns] = obuf[n, t, :, columns]
    for v in range(4):
        ho = lax.rem(11 - 2 * zl - c, 4)
        n = lax.rem(v - ho + 4, 4) * 4 + ho
        for t in range(2):
            last = obuf_one[n, t].astype(F32)
            for k in range(11):
                out[t, v, 48:49, 128 * k : 128 * k + 128] = last[k : k + 1, :].astype(BF16)

    for part in range(len(PARTS)):
        all_back(part, lambda made: made.wait_send())


def body(
    tokens, tile_of_slot, shifts, norm_gain_space, norm_bias_space, w_qkv_space, w_out_space,
    norm_gain_time, norm_bias_time, w_qkv_time, w_out_time,
):
    smem = pl.BlockSpec(memory_space=pltpu.SMEM)
    vmem = pl.BlockSpec(memory_space=pltpu.VMEM)
    anywhere = pl.BlockSpec(memory_space=pl.ANY)
    dma = pltpu.SemaphoreType.DMA
    encoded = pl.pallas_call(
        kernel,
        out_shape=jax.ShapeDtypeStruct((2, 4, 49, D), BF16),
        in_specs=[smem, smem, anywhere] + [vmem] * 8,
        out_specs=vmem,
        scratch_shapes=[
            pltpu.VMEM((4, D, EP), BF16),
            pltpu.VMEM((4, D, EP), BF16),
            pltpu.VMEM((88, EP), BF16),
            pltpu.VMEM((88, EP), BF16),
            pltpu.VMEM((2, 88, EP), BF16),
            pltpu.VMEM((2, 88, EP), BF16),
            pltpu.VMEM((16, 49, D), BF16),
            pltpu.VMEM((16, 64, D), BF16),
            pltpu.VMEM((ROWS, 1024), BF16),
            pltpu.VMEM((400, 2 * ROWS), BF16),
            pltpu.VMEM((TROWS, D), BF16),
            pltpu.VMEM((TROWS, D), BF16),
            pltpu.VMEM((3, TROWS, EP), BF16),
            pltpu.VMEM((TROWS, EP), BF16),
            pltpu.VMEM((2, ROWS, D), BF16),
            pltpu.VMEM((24, 16, D), BF16),
            pltpu.VMEM((32, 16, D), BF16),
            pltpu.VMEM((32, 16, D), BF16),
            pltpu.VMEM((16, 2, 16, D), BF16),
            pltpu.VMEM((8, 16, 128), BF16),
            pltpu.VMEM((32, 16, 128), BF16),
            pltpu.VMEM((32, 16, 128), BF16),
            pltpu.VMEM((16, 2, 16, 128), BF16),
            pltpu.VMEM((32, 16, 128), F32),
            pltpu.VMEM((TROWS, TROWS), BF16),
            dma((2, 3)), dma((2, 2)), dma((2,)), dma((COPIES[0],)), dma((COPIES[0],)), dma((COPIES[1],)), dma((COPIES[1],)),
            dma((15,)), dma((16,)), dma, dma((2,)), dma((2,)),
            dma((2, 32)), dma((2, 32)), dma, dma((2, 16)), dma((2, 16)), dma,
        ],
        compiler_params=pltpu.CompilerParams(
            collective_id=0, has_side_effects=True, vmem_limit_bytes=60 * 1024 * 1024
        ),
        cost_estimate=pl.CostEstimate(flops=12_000_000_000, bytes_accessed=40_000_000, transcendentals=2_000_000),
    )(
        tile_of_slot, shifts.T, tokens.reshape(8, 49, D), w_qkv_space, w_out_space.T, w_qkv_time, w_out_time.T,
        norm_gain_space, norm_bias_space, norm_gain_time, norm_bias_time,
    )
    return encoded.reshape(tokens.shape)


def solution(mesh):
    placed = (
        P("tm", "space", None, None, None), P(), P(), P(), P(), P("tm", None), P(None, "tm"),
        P(), P(), P("tm", None), P(None, "tm"),
    )
    return jax.shard_map(
        body,
        mesh=mesh,
        in_specs=placed,
        out_specs=P("tm", "space", None, None, None),
        check_vma=False,
    )
```

```python
import functools

import jax
import jax.numpy as jnp
from jax import lax
from jax.experimental import pallas as pl
from jax.experimental.pallas import tpu as pltpu
from jax.sharding import PartitionSpec as P

HEADS = 12
HEAD_DIM = 88
D = 1408
E = 1056
EP = 1152
WIN = 208
ROWS = 2 * WIN
TROWS = 512
EPSILON = 1e-06
SCALE = HEAD_DIM ** (-0.5)
MESH = pl.DeviceIdType.MESH
F32 = jnp.float32
BF16 = jnp.bfloat16
COPIES = (72, 72)
PARTS = ((0, 768), (768, 640))


def div(values, by):
    return lax.shift_right_logical(values * (-(-65536 // by)), 16)


def mod(values, by):
    return values - by * div(values, by)


def wrap(values, size):
    return values - jnp.where(values >= size, size, 0)


def iota(shape, axis):
    return lax.broadcasted_iota(jnp.int32, shape, axis)


def one_hot(index, columns):
    hit = index == iota((index.shape[0], columns), 1)
    return jnp.where(hit, F32(1.0), F32(0.0)).astype(BF16)


def matmul(left, right):
    return jnp.dot(left, right, preferred_element_type=F32)


def matmul_nt(left, right):
    return lax.dot_general(left, right, (((1,), (1,)), ((), ())), preferred_element_type=F32)


def normalize(source, target, gain_ref, bias_ref, count, valid):
    def one(n, carry):
        rows = pl.ds(pl.multiple_of(n * 32, 32), 32)
        widened = source[rows, :].astype(F32)
        average = jnp.mean(widened, axis=-1, keepdims=True)
        centered = widened - average
        variance = jnp.mean(centered * centered, axis=-1, keepdims=True)
        normed = centered * lax.rsqrt(variance + EPSILON) * gain_ref[...] + bias_ref[...]
        keep = valid(n * 32 + iota((32, 1), 0))
        target[rows, :] = jnp.where(keep, normed, F32(0.0)).astype(BF16)
        return carry

    lax.fori_loop(0, count // 32, one, 0)


def project(normed, full, qkv, kind, rows):
    qkv[kind, rows, :] = matmul(normed[rows, :], full[kind]).astype(BF16)


def attend(qkv, mix, rows, allowed):
    count = allowed.shape[0]
    partial = None
    for head in range(HEADS):
        low = HEAD_DIM * head
        first = low // 128 * 128
        last = -(-(low + HEAD_DIM) // 128) * 128
        lane = first + iota((count, last - first), 1)
        own = (lane >= low) & (lane < low + HEAD_DIM)
        zero = jnp.zeros((count, last - first), BF16)
        query = qkv[0, rows, first:last]
        keys = jnp.where(own, qkv[1, rows, first:last], zero)
        values = jnp.where(own, qkv[2, rows, first:last], zero)
        weights = jnp.where(allowed, jnp.exp(matmul_nt(query, keys) * SCALE), F32(0.0))
        total = jnp.sum(weights, axis=-1, keepdims=True)
        shares = (weights * (1.0 / total)).astype(BF16)
        mixed = matmul(shares, values)
        pieces = [mixed[:, n : n + 128] for n in range(0, last - first, 128)]
        if partial is not None:
            pieces[0] = pieces[0] + partial
        partial = None
        if head < HEADS - 1 and (low + HEAD_DIM) % 128:
            partial = pieces.pop()
        for n, piece in enumerate(pieces):
            mix[rows, first + 128 * n : first + 128 * n + 128] = piece.astype(BF16)


def out_project(mix, full, residual, columns, rows):
    product = matmul_nt(mix[rows, :], full[3, columns, :])
    return (residual[rows, columns].astype(F32) + product).astype(BF16)


def stage_shard(place, w_qkv, w_out, staged):
    x = place[2]
    staged[...] = jnp.zeros_like(staged)
    for kind in range(3):
        @pl.when(x == kind)
        def _():
            staged[:, :E] = w_qkv[:, E * kind : E * kind + E]

    @pl.when(x == 3)
    def _():
        staged[:, :E] = w_out[...]


def gather_steps(place, sizes, staged, zbuf, full, z_send, z_recv, z_local, send_sem, recv_sem, pending):
    y, zh, x, zl, c = place
    dev = device
    core_of = lax.div(zh, 2)
    is_sender = core_of == c
    mine = lax.rem(zh, 2)

    def z_copy(step):
        return pltpu.make_async_remote_copy(
            src_ref=staged,
            dst_ref=zbuf.at[mine],
            send_sem=z_send.at[step - 1],
            recv_sem=z_recv.at[mine],
            device_id=dev(y, lax.rem(zh + step, 4), x, zl, c),
            device_id_type=MESH,
        )

    def z_own():
        return pltpu.make_async_copy(staged, zbuf.at[mine], z_local)

    @pl.when(is_sender)
    def _():
        for step in (1, 3, 2):
            z_copy(step).start()
        z_own().start()

    def z_finish():
        @pl.when(is_sender)
        def _():
            for step in (1, 3, 2):
                z_copy(step).wait_send()

    pending.append(z_finish)
    yield

    for k in range(2):
        @pl.when(zh != 2 * c + k)
        def _():
            pltpu.make_async_remote_copy(
                src_ref=staged,
                dst_ref=zbuf.at[k],
                send_sem=z_send.at[0],
                recv_sem=z_recv.at[k],
                device_id=dev(y, zh, x, zl, 1 - c),
                device_id_type=MESH,
            ).wait_recv()

    @pl.when(is_sender)
    def _():
        z_own().wait()

    def region(kind, row, core, low, count):
        start = pl.multiple_of(352 * lax.rem(y + row + 4, 4) + 176 * core + low, 16)
        return full.at[lax.rem(x + kind + 4, 4), pl.ds(start, count), :]

    rows_a, rows_b, split_z = sizes
    low_a = (176 - rows_a) * zl if split_z else 0
    low_b = rows_a - (rows_a - 48) * zl if split_z else rows_a
    base = pl.multiple_of(352 * y + 176 * c, 16)
    both = jnp.concatenate([zbuf[0].astype(F32), zbuf[1].astype(F32)], axis=0)
    full[x, pl.ds(base, 176), :] = both.astype(BF16)

    xp, xm = dev(y, zh, lax.rem(x + 1, 4), zl, c), dev(y, zh, lax.rem(x + 3, 4), zl, c)
    yp, ym = dev(lax.rem(y + 1, 4), zh, x, zl, c), dev(lax.rem(y + 3, 4), zh, x, zl, c)
    sibling = dev(y, zh, x, zl, 1 - c)
    counter = [0]

    def copy(k, piece, target):
        return pltpu.make_async_remote_copy(
            src_ref=piece,
            dst_ref=piece,
            send_sem=send_sem.at[k],
            recv_sem=recv_sem.at[k],
            device_id=target,
            device_id_type=MESH,
        )

    def send(piece, target):
        k = counter[0]
        counter[0] += 1
        made = copy(k, piece, target)
        made.start()
        pending.append(made.wait_send)
        return k

    def recv(k, piece):
        copy(k, piece, sibling).wait_recv()

    def part_a(kind, row, low=0, count=rows_a, core=c):
        return region(kind, row, core, low_a + low, count)

    def part_b(kind, row, low=0, count=rows_b, core=c):
        return region(kind, row, core, low_b + low, count)

    def part_z(kind, row, parity, low=0, count=48, core=c):
        return region(kind, row, core, 128 * parity + low, count)

    arriving = []
    half_a = 16 * ((rows_a // 16 + 1) // 2)
    half_b = 16 * ((rows_b // 16 + 1) // 2)

    inner = dev(y, zh, x, 1 - zl, c)
    outer = dev(y, lax.rem(zh + 2 * zl + 3, 4), x, 1 - zl, c)
    crossing = []

    def share(part, kind, row):
        arriving.append((send(part(kind, row), sibling), part(kind, row, core=1 - c)))
        if not split_z or part is not part_a:
            return
        if kind == 0 and row == 0:
            k = send(part_z(0, 0, 1 - zl), sibling)
            arriving.append((k, part_z(0, 0, 1 - zl, core=1 - c)))
        else:
            k_out = send(part_z(kind, row, zl, 0, 32), outer)
            k_in = send(part_z(kind, row, zl, 32, 16), inner)
            crossing.append((kind, row, k_out, k_in))

    def crossed(count):
        for kind, row, k_out, k_in in crossing[:count]:
            recv(k_out, part_z(kind, row, 1 - zl, 0, 32))
            recv(k_in, part_z(kind, row, 1 - zl, 32, 16))
            k = send(part_z(kind, row, 1 - zl), sibling)
            arriving.append((k, part_z(kind, row, 1 - zl, core=1 - c)))
        del crossing[:count]

    class Ring:
        def __init__(self, part, along_x, at, plus, minus, halves):
            self.part, self.along_x, self.at = part, along_x, at
            self.plus, self.minus, self.halves = plus, minus, halves
            own = self.piece(0)
            self.k_plus = send(own, plus)
            self.k_minus = send(own, minus)

        def spot(self, step):
            return (step, self.at) if self.along_x else (self.at, step)

        def piece(self, step, *cut):
            return self.part(*self.spot(step), *cut)

        def near(self):
            low, high = self.halves
            recv(self.k_plus, self.piece(-1))
            self.f_plus = send(self.piece(-1, 0, low), self.plus)
            recv(self.k_minus, self.piece(1))
            self.f_minus = send(self.piece(1, low, high), self.minus)

        def far(self):
            low, high = self.halves
            recv(self.f_plus, self.piece(2, 0, low))
            recv(self.f_minus, self.piece(2, low, high))

    def ring_a1():
        return Ring(part_a, True, 0, xp, xm, (half_a, rows_a - half_a))

    def ring_b1():
        return Ring(part_b, False, 0, yp, ym, (half_b, rows_b - half_b))

    def ring_a2(kind):
        return Ring(part_a, False, kind, yp, ym, (half_a, rows_a - half_a))

    def ring_b2(row):
        return Ring(part_b, True, row, xp, xm, (half_b, rows_b - half_b))

    a1, b1 = ring_a1(), ring_b1()
    seconds = [ring_a2(0), ring_b2(0)]
    share(part_a, 0, 0)
    share(part_b, 0, 0)
    yield
    a1.near()
    b1.near()
    for step in (-1, 1):
        seconds += [ring_a2(step), ring_b2(step)]
    for step in (-1, 1):
        share(part_a, step, 0)
        share(part_b, 0, step)
    yield
    a1.far()
    b1.far()
    seconds += [ring_a2(2), ring_b2(2)]
    share(part_a, 2, 0)
    share(part_b, 0, 2)
    yield
    for n in range(0, 8, 2):
        for ring in seconds[n : n + 2]:
            ring.near()
            for step in (-1, 1):
                share(ring.part, *ring.spot(step))
        yield
    for n in range(0, 8, 2):
        for ring in seconds[n : n + 2]:
            ring.far()
            share(ring.part, *ring.spot(2))
        if n < 6:
            yield
    yield
    crossed(len(crossing))
    for k, piece in arriving:
        recv(k, piece)
    assert counter[0] == send_sem.shape[0], counter
    yield


def device(y, zh, x, zl, c):
    return (y * 4 + zh, x * 4 + zl * 2 + c)


def advance(steps):
    next(steps, None)


def kernel(
    slots, shifts, tokens, w_qkv1, w_out1, w_qkv2, w_out2, gain1, bias1, gain2, bias2, out,
    full1, full2, staged1, staged2, zbuf1, zbuf2, tiles, frames, p_in, p_out, xw, xn, qkv, mix, mid2, snd, rbuf, ret, obuf,
    snd_one, rbuf_one, ret_one, obuf_one, wide, by_time,
    z_send, z_recv, z_local, g_send1, g_recv1, g_send2, g_recv2, e1_send, e1_recv, e1_local, m_send, m_recv,
    e2_send, e2_recv, e2_local, e3_send, e3_recv, e3_local,
):
    tm, space = lax.axis_index("tm"), lax.axis_index("space")
    y, zh = lax.div(tm, 4), lax.rem(tm, 4)
    x, zl, c = lax.div(space, 4), lax.rem(lax.div(space, 2), 2), lax.rem(space, 2)
    place = (y, zh, x, zl, c)
    sibling = device(y, zh, x, zl, 1 - c)
    video_t = lax.rem(zh + y, 4)
    is_self = video_t == x
    quarter = lax.rem(zh + 2 * zl + c, 4)
    single = quarter == 3
    pending = []

    barrier = pltpu.get_barrier_semaphore()

    def greet(target):
        pl.semaphore_signal(barrier, inc=1, device_id=target, device_id_type=MESH)

    greet(sibling)
    for step in range(1, 8):
        greet(device(y, zh, lax.rem(x + step // 2, 4), lax.rem(zl + step % 2, 2), c))

    def greet_times(n, carry):
        other = lax.rem(tm + n, 16)
        greet((other, space))
        return carry

    lax.fori_loop(1, 16, greet_times, 0)

    def greet_sources(n, carry):
        other = lax.rem(tm + lax.div(n, 2), 16)
        zl_other = lax.rem(zl + lax.rem(n, 2), 2)

        @pl.when(jnp.logical_not(is_self & (n == 0)))
        def _():
            greet((other, video_t * 4 + zl_other * 2 + c))

        return carry

    lax.fori_loop(0, 32, greet_sources, 0)
    greet(device(y, lax.rem(zh + 2 * zl + 3, 4), x, 1 - zl, c))
    stage_shard(place, w_qkv1, w_out1, staged1)
    pl.semaphore_wait(barrier, 56 - jnp.where(is_self, 1, 0))

    g1 = gather_steps(
        place, (96, 80, False), staged1, zbuf1, full1, z_send.at[0], z_recv.at[0], z_local.at[0],
        g_send1, g_recv1, pending,
    )
    g2 = gather_steps(
        place, (96, 80, False), staged2, zbuf2, full2, z_send.at[1], z_recv.at[1], z_local.at[1],
        g_send2, g_recv2, pending,
    )
    advance(g1)

    own_tile = pltpu.make_async_copy(tokens.at[zl * 4 + x], tiles.at[space], e1_local)
    own_tile.start()
    def send_tiles(steps):
        for step in steps:
            xo, zo = lax.rem(x + step // 2, 4), lax.rem(zl + step % 2, 2)
            made = pltpu.make_async_remote_copy(
                src_ref=tokens.at[zo * 4 + xo],
                dst_ref=tiles.at[space],
                send_sem=e1_send.at[step - 1],
                recv_sem=e1_recv.at[space],
                device_id=device(y, zh, xo, zo, c),
                device_id_type=MESH,
            )
            made.start()
            pending.append(made.wait_send)

    send_tiles((2, 6, 4))
    stage_shard(place, w_qkv2, w_out2, staged2)
    wide[...] = jnp.zeros_like(wide)
    frames[...] = jnp.zeros_like(frames)
    shift_r, shift_c = shifts[0, x], shifts[1, x]

    row = iota((ROWS, 1), 0)
    wc = div(row, WIN)
    spot = row - wc * WIN
    pr = div(spot, 14)
    pc = spot - 14 * pr
    r = wrap(14 * c + pr + shift_r, 28)
    col = wrap(14 * wc + pc + shift_c, 28)
    tile = 4 * div(r, 7) + div(col, 7)
    slot = jnp.zeros_like(tile)
    for s in range(16):
        slot = jnp.where(tile == slots[s], s, slot)
    index = slot * 64 + mod(r, 7) * 7 + mod(col, 7)
    p_in[...] = one_hot(jnp.where(spot < 196, index, -1), 1024)

    advance(g1)
    send_tiles((1, 3, 7, 5))
    advance(g2)

    row = iota((400, 1), 0)
    last = row >= 384
    slot8 = jnp.where(last, row - 384, div(row, 48))
    j = jnp.where(last, 48, row - 48 * slot8)
    tile = jnp.zeros_like(row)
    for n in range(8):
        tile = jnp.where(slot8 == n, slots[4 * (n // 2) + 2 * (n % 2) + c], tile)
    jr = div(j, 7)
    r = 7 * div(tile, 4) + jr
    col = 7 * mod(tile, 4) + (j - 7 * jr)
    sr = wrap(r + 28 - shift_r, 28)
    sc = wrap(col + 28 - shift_c, 28)
    wr, wc = div(sr, 14), div(sc, 14)
    index = wr * ROWS + wc * WIN + (sr - 14 * wr) * 14 + (sc - 14 * wc)
    p_out[...] = one_hot(jnp.where(slot8 < 8, index, -1), 2 * ROWS)

    advance(g1)

    own_tile.wait()

    def tile_copy(s, n):
        return pltpu.make_async_remote_copy(
            src_ref=tiles.at[s],
            dst_ref=tiles.at[s],
            send_sem=e1_send.at[7 + n],
            recv_sem=e1_recv.at[s],
            device_id=sibling,
            device_id_type=MESH,
        )

    for n, step in enumerate((0, 2, 6, 1, 3, 7, 4, 5)):
        xo, zo = lax.rem(x + step // 2, 4), lax.rem(zl + step % 2, 2)
        s = xo * 4 + zo * 2 + c
        made = tile_copy(s, n)
        if step:
            made.wait_recv()
        made.start()
        pending.append(made.wait_send)
    advance(g1)
    advance(g1)
    for step in range(8):
        s = 4 * (step // 2) + 2 * (step % 2) + 1 - c
        tile_copy(s, 0).wait_recv()

    def widen(s, carry):
        frames[s, :49, :] = tiles[s]
        return carry

    lax.fori_loop(0, 16, widen, 0)
    for first, width in PARTS:
        columns = slice(first, first + width)
        cells = frames[:, :, columns].reshape(1024, width)
        xw[:ROWS, columns] = matmul(p_in[...], cells).astype(BF16)
        advance(g1)

    def in_window(rows):
        return rows - jnp.where(rows >= WIN, WIN, 0) < 196

    normalize(xw, xn, gain1, bias1, ROWS, in_window)
    for n in range(5):
        advance(g1)
    advance(g2)
    advance(g1)
    for kind in range(3):
        project(xn, full1, qkv, kind, slice(0, ROWS))
        if kind:
            advance(g2)

    def regions(shape, axis, column):
        at = iota(shape, axis)
        down = div(at, 14)
        across = at - 14 * down
        kind = 2 * jnp.where(14 * c + down >= 28 - shift_r, 1, 0)
        kind = kind + jnp.where(14 * column + across >= 28 - shift_c, 1, 0)
        return jnp.where(at < 196, kind, -1)

    for column in range(2):
        allowed = regions((WIN, 1), 0, column) == regions((1, WIN), 1, column)
        attend(qkv, mix, pl.ds(column * WIN, WIN), allowed)
        advance(g2)

    def swap(n, core):
        first, width = PARTS[n]
        piece = mid2.at[core, :, pl.ds(first, width)]
        return pltpu.make_async_remote_copy(
            src_ref=piece,
            dst_ref=piece,
            send_sem=m_send.at[n],
            recv_sem=m_recv.at[n],
            device_id=sibling,
            device_id_type=MESH,
        )

    for n, (first, width) in enumerate(PARTS):
        mid2[c, :, first : first + width] = out_project(mix, full1, xw, slice(first, first + width), slice(0, ROWS))
        swap(n, c).start()
        pending.append(swap(n, c).wait_send)
        advance(g2)

    time = 2 * tm + zl

    def row_target(n):
        dx, dz, dh = lax.div(n, 8), lax.rem(lax.div(n, 4), 2), lax.rem(n, 4)
        xo, zo, ho = lax.rem(x + dx, 4), lax.rem(zl + dz, 2), lax.rem(zh + dh, 4)
        target = device(lax.rem(x - ho + 4, 4), ho, xo, zo, c)
        return xo * 2 + zo, lax.rem(ho + 2 * zo + c, 4), target

    def row_copy(n, part):
        s, q, target = row_target(n)
        columns = pl.ds(*PARTS[part])
        return pltpu.make_async_remote_copy(
            src_ref=snd.at[s * 3 + q, :, columns],
            dst_ref=rbuf.at[time, :, columns],
            send_sem=e2_send.at[part, n],
            recv_sem=e2_recv.at[part, time],
            device_id=target,
            device_id_type=MESH,
        )

    def one_copy(n):
        s, q, target = row_target(n)
        return pltpu.make_async_remote_copy(
            src_ref=snd_one.at[s],
            dst_ref=rbuf_one.at[time],
            send_sem=e2_send.at[1, n],
            recv_sem=e2_recv.at[1, time],
            device_id=target,
            device_id_type=MESH,
        )

    def each_row(n, part, do):
        away = jnp.logical_not(is_self & (n == 0))
        q = row_target(n)[1]

        @pl.when(away & (q < 3))
        def _():
            do(row_copy(n, part))

        if part:
            @pl.when(away & (q == 3))
            def _():
                do(one_copy(n))

    for part, (first, width) in enumerate(PARTS):
        columns = slice(first, first + width)
        swap(part, 1 - c).wait_recv()
        cells = mid2[:, :, columns].reshape(2 * ROWS, width)
        moved = matmul(p_out[...], cells)
        snd[:, :, columns] = moved[:384].astype(BF16).reshape(24, 16, width)
        for n in range(width // 128):
            wide[:8, first // 128 + n, :] = moved[384:392, 128 * n : 128 * n + 128]
        if part:
            snd_one[...] = wide[:8].astype(BF16)

        def start_rows(n, carry):
            each_row(n, part, lambda made: made.start())
            return carry

        lax.fori_loop(0, 32, start_rows, 0)

    @pl.when(is_self & jnp.logical_not(single))
    def _():
        own_rows = pltpu.make_async_copy(snd.at[(x * 2 + zl) * 3 + quarter], rbuf.at[time], e2_local)
        own_rows.start()
        own_rows.wait()

    @pl.when(is_self & single)
    def _():
        own_rows = pltpu.make_async_copy(snd_one.at[x * 2 + zl], rbuf_one.at[time], e2_local)
        own_rows.start()
        own_rows.wait()

    for n in range(8):
        advance(g2)

    row = iota((TROWS, 1), 0)
    at = div(row, 32)
    by_position = one_hot((row - 32 * at) * 16 + at, TROWS)

    row = iota((256, 1), 0)
    at = div(row, 8)
    by_time[...] = one_hot((row - 8 * at) * 32 + at, 256)

    def wait_landed(piece, part, n):
        pltpu.make_async_remote_copy(
            src_ref=piece,
            dst_ref=piece,
            send_sem=e2_send.at[part, 0],
            recv_sem=e2_recv.at[part, n],
            device_id=sibling,
            device_id_type=MESH,
        ).wait_recv()

    @pl.when(jnp.logical_not(single))
    def _():
        for part, (first, width) in enumerate(PARTS):
            columns = slice(first, first + width)

            def wait_rows(n, carry):
                @pl.when(jnp.logical_not(is_self & (n == time)))
                def _():
                    wait_landed(rbuf.at[n, :, pl.ds(first, width)], part, n)

                return carry

            lax.fori_loop(0, 32, wait_rows, 0)
            cells = rbuf[:, :, columns].reshape(TROWS, width)
            xw[:, columns] = matmul(by_position, cells).astype(BF16)

    @pl.when(single)
    def _():
        def wait_ones(n, carry):
            @pl.when(jnp.logical_not(is_self & (n == time)))
            def _():
                wait_landed(rbuf_one.at[n], 1, n)

            return carry

        lax.fori_loop(0, 32, wait_ones, 0)
        xw[...] = jnp.zeros_like(xw)
        wide[...] = rbuf_one[...].astype(F32)
        for n in range(11):
            xw[:32, 128 * n : 128 * n + 128] = wide[:, n, :].astype(BF16)

    normalize(xw, xn, gain2, bias2, TROWS, lambda rows: jnp.logical_not(single) | (rows < 32))
    advance(g2)
    def back_copy(n, half):
        other = lax.rem(tm + n, 16)
        return pltpu.make_async_remote_copy(
            src_ref=ret.at[half, other],
            dst_ref=obuf.at[tm, half],
            send_sem=e3_send.at[half, n],
            recv_sem=e3_recv.at[half, tm],
            device_id=(other, space),
            device_id_type=MESH,
        )

    def back_one(n):
        other = lax.rem(tm + n, 16)
        return pltpu.make_async_remote_copy(
            src_ref=ret_one.at[pl.ds(2 * other, 2)],
            dst_ref=obuf_one.at[tm],
            send_sem=e3_send.at[0, n],
            recv_sem=e3_recv.at[0, tm],
            device_id=(other, space),
            device_id_type=MESH,
        )

    def all_back(half, do):
        @pl.when(jnp.logical_not(single))
        def _():
            def one(n, carry):
                do(back_copy(n, half))
                return carry

            lax.fori_loop(1, 16, one, 0)

        if half == 0:
            @pl.when(single)
            def _():
                def one(n, carry):
                    do(back_one(n))
                    return carry

                lax.fori_loop(1, 16, one, 0)

    for half in range(2):
        part_rows = slice(256 * half, 256 * half + 256)
        for kind in range(3):
            project(xn, full2, qkv, kind, part_rows)

        def attend_group(n, carry):
            left, right = iota((128, 1), 0), iota((1, 128), 1)
            rows = pl.ds(pl.multiple_of(n * 128, 128), 128)
            attend(qkv, mix, rows, div(left, 32) == div(right, 32))
            return carry

        lax.fori_loop(2 * half, 2 * half + 2, attend_group, 0)
        for first, width in PARTS:
            columns = slice(first, first + width)
            encoded = out_project(mix, full2, xw, columns, part_rows)
            ret[half, :, :, columns] = matmul(by_time[...], encoded).astype(BF16).reshape(16, 16, width)
            if half == 0:
                for n in range(width // 128):
                    wide[:, first // 128 + n, :] = encoded[:32, 128 * n : 128 * n + 128].astype(F32)
        if half == 0:
            ret_one[...] = wide[...].astype(BF16)
        all_back(half, lambda made: made.start())

    @pl.when(jnp.logical_not(single))
    def _():
        own_back = pltpu.make_async_copy(ret.at[:, tm], obuf.at[tm], e3_local)
        own_back.start()
        own_back.wait()

    @pl.when(single)
    def _():
        own_back = pltpu.make_async_copy(ret_one.at[pl.ds(2 * tm, 2)], obuf_one.at[tm], e3_local)
        own_back.start()
        own_back.wait()

    for finish in pending:
        finish()

    for part in range(len(PARTS)):
        def finish_rows(n, carry):
            each_row(n, part, lambda made: made.wait_send())
            return carry

        lax.fori_loop(0, 32, finish_rows, 0)

    def wait_back(piece, part, n):
        pltpu.make_async_remote_copy(
            src_ref=piece,
            dst_ref=piece,
            send_sem=e3_send.at[part, 0],
            recv_sem=e3_recv.at[part, n],
            device_id=sibling,
            device_id_type=MESH,
        ).wait_recv()

    for half in range(2):
        def land(n, carry):
            q = lax.rem(lax.rem(n, 4) + 2 * zl + c, 4)

            @pl.when((n != tm) & (q < 3))
            def _():
                wait_back(obuf.at[n, half], half, n)

            if half == 0:
                @pl.when((n != tm) & (q == 3))
                def _():
                    wait_back(obuf_one.at[n], half, n)

            return carry

        lax.fori_loop(0, 16, land, 0)
    for q in range(3):
        for v in range(4):
            ho = lax.rem(q + 8 - 2 * zl - c, 4)
            n = lax.rem(v - ho + 4, 4) * 4 + ho
            early, late = obuf[n, 0].astype(F32), obuf[n, 1].astype(F32)
            for t in range(2):
                rows = jnp.concatenate([early[8 * t : 8 * t + 8], late[8 * t : 8 * t + 8]], axis=0)
                out[t, v, 16 * q : 16 * q + 16, :] = rows.astype(BF16)
    for v in range(4):
        ho = lax.rem(11 - 2 * zl - c, 4)
        n = lax.rem(v - ho + 4, 4) * 4 + ho
        for t in range(2):
            last = obuf_one[n, t].astype(F32)
            for k in range(11):
                out[t, v, 48:49, 128 * k : 128 * k + 128] = last[k : k + 1, :].astype(BF16)

    for half in range(2):
        all_back(half, lambda made: made.wait_send())


def body(
    tokens, tile_of_slot, shifts, norm_gain_space, norm_bias_space, w_qkv_space, w_out_space,
    norm_gain_time, norm_bias_time, w_qkv_time, w_out_time,
):
    smem = pl.BlockSpec(memory_space=pltpu.SMEM)
    vmem = pl.BlockSpec(memory_space=pltpu.VMEM)
    anywhere = pl.BlockSpec(memory_space=pl.ANY)
    dma = pltpu.SemaphoreType.DMA
    encoded = pl.pallas_call(
        kernel,
        out_shape=jax.ShapeDtypeStruct((2, 4, 49, D), BF16),
        in_specs=[smem, smem, anywhere] + [vmem] * 8,
        out_specs=vmem,
        scratch_shapes=[
            pltpu.VMEM((4, D, EP), BF16),
            pltpu.VMEM((4, D, EP), BF16),
            pltpu.VMEM((88, EP), BF16),
            pltpu.VMEM((88, EP), BF16),
            pltpu.VMEM((2, 88, EP), BF16),
            pltpu.VMEM((2, 88, EP), BF16),
            pltpu.VMEM((16, 49, D), BF16),
            pltpu.VMEM((16, 64, D), BF16),
            pltpu.VMEM((ROWS, 1024), BF16),
            pltpu.VMEM((400, 2 * ROWS), BF16),
            pltpu.VMEM((TROWS, D), BF16),
            pltpu.VMEM((TROWS, D), BF16),
            pltpu.VMEM((3, TROWS, EP), BF16),
            pltpu.VMEM((TROWS, EP), BF16),
            pltpu.VMEM((2, ROWS, D), BF16),
            pltpu.VMEM((24, 16, D), BF16),
            pltpu.VMEM((32, 16, D), BF16),
            pltpu.VMEM((2, 16, 16, D), BF16),
            pltpu.VMEM((16, 2, 16, D), BF16),
            pltpu.VMEM((8, 16, 128), BF16),
            pltpu.VMEM((32, 16, 128), BF16),
            pltpu.VMEM((32, 16, 128), BF16),
            pltpu.VMEM((16, 2, 16, 128), BF16),
            pltpu.VMEM((32, 16, 128), F32),
            pltpu.VMEM((256, 256), BF16),
            dma((2, 3)), dma((2, 2)), dma((2,)), dma((COPIES[0],)), dma((COPIES[0],)), dma((COPIES[1],)), dma((COPIES[1],)),
            dma((15,)), dma((16,)), dma, dma((2,)), dma((2,)),
            dma((2, 32)), dma((2, 32)), dma, dma((2, 16)), dma((2, 16)), dma,
        ],
        compiler_params=pltpu.CompilerParams(
            collective_id=0, has_side_effects=True, vmem_limit_bytes=60 * 1024 * 1024
        ),
        cost_estimate=pl.CostEstimate(flops=12_000_000_000, bytes_accessed=40_000_000, transcendentals=2_000_000),
    )(
        tile_of_slot, shifts.T, tokens.reshape(8, 49, D), w_qkv_space, w_out_space.T, w_qkv_time, w_out_time.T,
        norm_gain_space, norm_bias_space, norm_gain_time, norm_bias_time,
    )
    return encoded.reshape(tokens.shape)


def solution(mesh):
    placed = (
        P("tm", "space", None, None, None), P(), P(), P(), P(), P("tm", None), P(None, "tm"),
        P(), P(), P("tm", None), P(None, "tm"),
    )
    return jax.shard_map(
        body,
        mesh=mesh,
        in_specs=placed,
        out_specs=P("tm", "space", None, None, None),
        check_vma=False,
    )
```

```python
import functools

import jax
import jax.numpy as jnp
from jax import lax
from jax.experimental import pallas as pl
from jax.experimental.pallas import tpu as pltpu
from jax.sharding import PartitionSpec as P

HEADS = 12
HEAD_DIM = 88
D = 1408
E = 1056
EP = 1152
WIN = 208
ROWS = 2 * WIN
TROWS = 512
EPSILON = 1e-06
SCALE = HEAD_DIM ** (-0.5)
MESH = pl.DeviceIdType.MESH
F32 = jnp.float32
BF16 = jnp.bfloat16
COPIES = (72, 72)
PARTS = ((0, 768), (768, 640))


def div(values, by):
    return lax.shift_right_logical(values * (-(-65536 // by)), 16)


def mod(values, by):
    return values - by * div(values, by)


def wrap(values, size):
    return values - jnp.where(values >= size, size, 0)


def iota(shape, axis):
    return lax.broadcasted_iota(jnp.int32, shape, axis)


def one_hot(index, columns):
    hit = index == iota((index.shape[0], columns), 1)
    return jnp.where(hit, F32(1.0), F32(0.0)).astype(BF16)


def matmul(left, right):
    return jnp.dot(left, right, preferred_element_type=F32)


def matmul_nt(left, right):
    return lax.dot_general(left, right, (((1,), (1,)), ((), ())), preferred_element_type=F32)


def normalize(source, target, gain_ref, bias_ref, count, valid):
    def one(n, carry):
        rows = pl.ds(pl.multiple_of(n * 32, 32), 32)
        widened = source[rows, :].astype(F32)
        average = jnp.mean(widened, axis=-1, keepdims=True)
        centered = widened - average
        variance = jnp.mean(centered * centered, axis=-1, keepdims=True)
        normed = centered * lax.rsqrt(variance + EPSILON) * gain_ref[...] + bias_ref[...]
        keep = valid(n * 32 + iota((32, 1), 0))
        target[rows, :] = jnp.where(keep, normed, F32(0.0)).astype(BF16)
        return carry

    lax.fori_loop(0, count // 32, one, 0)


def project(normed, full, qkv, kind, rows):
    qkv[kind, rows, :] = matmul(normed[rows, :], full[kind]).astype(BF16)


def attend(qkv, mix, rows, allowed):
    count = allowed.shape[0]
    partial = None
    for head in range(HEADS):
        low = HEAD_DIM * head
        first = low // 128 * 128
        last = -(-(low + HEAD_DIM) // 128) * 128
        lane = first + iota((count, last - first), 1)
        own = (lane >= low) & (lane < low + HEAD_DIM)
        zero = jnp.zeros((count, last - first), BF16)
        query = qkv[0, rows, first:last]
        keys = jnp.where(own, qkv[1, rows, first:last], zero)
        values = jnp.where(own, qkv[2, rows, first:last], zero)
        weights = jnp.where(allowed, jnp.exp(matmul_nt(query, keys) * SCALE), F32(0.0))
        total = jnp.sum(weights, axis=-1, keepdims=True)
        shares = (weights * (1.0 / total)).astype(BF16)
        mixed = matmul(shares, values)
        pieces = [mixed[:, n : n + 128] for n in range(0, last - first, 128)]
        if partial is not None:
            pieces[0] = pieces[0] + partial
        partial = None
        if head < HEADS - 1 and (low + HEAD_DIM) % 128:
            partial = pieces.pop()
        for n, piece in enumerate(pieces):
            mix[rows, first + 128 * n : first + 128 * n + 128] = piece.astype(BF16)


def out_project(mix, full, residual, columns, rows):
    product = matmul_nt(mix[rows, :], full[3, columns, :])
    return (residual[rows, columns].astype(F32) + product).astype(BF16)


def stage_shard(place, w_qkv, w_out, staged):
    x = place[2]
    staged[...] = jnp.zeros_like(staged)
    for kind in range(3):
        @pl.when(x == kind)
        def _():
            staged[:, :E] = w_qkv[:, E * kind : E * kind + E]

    @pl.when(x == 3)
    def _():
        staged[:, :E] = w_out[...]


def gather_steps(place, sizes, staged, zbuf, full, z_send, z_recv, z_local, send_sem, recv_sem, pending):
    y, zh, x, zl, c = place
    dev = device
    core_of = lax.div(zh, 2)
    is_sender = core_of == c
    mine = lax.rem(zh, 2)

    def z_copy(step):
        return pltpu.make_async_remote_copy(
            src_ref=staged,
            dst_ref=zbuf.at[mine],
            send_sem=z_send.at[step - 1],
            recv_sem=z_recv.at[mine],
            device_id=dev(y, lax.rem(zh + step, 4), x, zl, c),
            device_id_type=MESH,
        )

    def z_own():
        return pltpu.make_async_copy(staged, zbuf.at[mine], z_local)

    @pl.when(is_sender)
    def _():
        for step in (1, 3, 2):
            z_copy(step).start()
        z_own().start()

    def z_finish():
        @pl.when(is_sender)
        def _():
            for step in (1, 3, 2):
                z_copy(step).wait_send()

    pending.append(z_finish)
    yield

    for k in range(2):
        @pl.when(zh != 2 * c + k)
        def _():
            pltpu.make_async_remote_copy(
                src_ref=staged,
                dst_ref=zbuf.at[k],
                send_sem=z_send.at[0],
                recv_sem=z_recv.at[k],
                device_id=dev(y, zh, x, zl, 1 - c),
                device_id_type=MESH,
            ).wait_recv()

    @pl.when(is_sender)
    def _():
        z_own().wait()

    def region(kind, row, core, low, count):
        start = pl.multiple_of(352 * lax.rem(y + row + 4, 4) + 176 * core + low, 16)
        return full.at[lax.rem(x + kind + 4, 4), pl.ds(start, count), :]

    rows_a, rows_b, split_z = sizes
    low_a = (176 - rows_a) * zl if split_z else 0
    low_b = rows_a - (rows_a - 48) * zl if split_z else rows_a
    base = pl.multiple_of(352 * y + 176 * c, 16)
    both = jnp.concatenate([zbuf[0].astype(F32), zbuf[1].astype(F32)], axis=0)
    full[x, pl.ds(base, 176), :] = both.astype(BF16)

    xp, xm = dev(y, zh, lax.rem(x + 1, 4), zl, c), dev(y, zh, lax.rem(x + 3, 4), zl, c)
    yp, ym = dev(lax.rem(y + 1, 4), zh, x, zl, c), dev(lax.rem(y + 3, 4), zh, x, zl, c)
    sibling = dev(y, zh, x, zl, 1 - c)
    counter = [0]

    def copy(k, piece, target):
        return pltpu.make_async_remote_copy(
            src_ref=piece,
            dst_ref=piece,
            send_sem=send_sem.at[k],
            recv_sem=recv_sem.at[k],
            device_id=target,
            device_id_type=MESH,
        )

    def send(piece, target):
        k = counter[0]
        counter[0] += 1
        made = copy(k, piece, target)
        made.start()
        pending.append(made.wait_send)
        return k

    def recv(k, piece):
        copy(k, piece, sibling).wait_recv()

    def part_a(kind, row, low=0, count=rows_a, core=c):
        return region(kind, row, core, low_a + low, count)

    def part_b(kind, row, low=0, count=rows_b, core=c):
        return region(kind, row, core, low_b + low, count)

    def part_z(kind, row, parity, low=0, count=48, core=c):
        return region(kind, row, core, 128 * parity + low, count)

    arriving = []
    half_a = 16 * ((rows_a // 16 + 1) // 2)
    half_b = 16 * ((rows_b // 16 + 1) // 2)

    inner = dev(y, zh, x, 1 - zl, c)
    outer = dev(y, lax.rem(zh + 2 * zl + 3, 4), x, 1 - zl, c)
    crossing = []

    def share(part, kind, row):
        arriving.append((send(part(kind, row), sibling), part(kind, row, core=1 - c)))
        if not split_z or part is not part_a:
            return
        if kind == 0 and row == 0:
            k = send(part_z(0, 0, 1 - zl), sibling)
            arriving.append((k, part_z(0, 0, 1 - zl, core=1 - c)))
        else:
            k_out = send(part_z(kind, row, zl, 0, 32), outer)
            k_in = send(part_z(kind, row, zl, 32, 16), inner)
            crossing.append((kind, row, k_out, k_in))

    def crossed(count):
        for kind, row, k_out, k_in in crossing[:count]:
            recv(k_out, part_z(kind, row, 1 - zl, 0, 32))
            recv(k_in, part_z(kind, row, 1 - zl, 32, 16))
            k = send(part_z(kind, row, 1 - zl), sibling)
            arriving.append((k, part_z(kind, row, 1 - zl, core=1 - c)))
        del crossing[:count]

    class Ring:
        def __init__(self, part, along_x, at, plus, minus, halves):
            self.part, self.along_x, self.at = part, along_x, at
            self.plus, self.minus, self.halves = plus, minus, halves
            own = self.piece(0)
            self.k_plus = send(own, plus)
            self.k_minus = send(own, minus)

        def spot(self, step):
            return (step, self.at) if self.along_x else (self.at, step)

        def piece(self, step, *cut):
            return self.part(*self.spot(step), *cut)

        def near(self):
            low, high = self.halves
            recv(self.k_plus, self.piece(-1))
            self.f_plus = send(self.piece(-1, 0, low), self.plus)
            recv(self.k_minus, self.piece(1))
            self.f_minus = send(self.piece(1, low, high), self.minus)

        def far(self):
            low, high = self.halves
            recv(self.f_plus, self.piece(2, 0, low))
            recv(self.f_minus, self.piece(2, low, high))

    def ring_a1():
        return Ring(part_a, True, 0, xp, xm, (half_a, rows_a - half_a))

    def ring_b1():
        return Ring(part_b, False, 0, yp, ym, (half_b, rows_b - half_b))

    def ring_a2(kind):
        return Ring(part_a, False, kind, yp, ym, (half_a, rows_a - half_a))

    def ring_b2(row):
        return Ring(part_b, True, row, xp, xm, (half_b, rows_b - half_b))

    a1, b1 = ring_a1(), ring_b1()
    seconds = [ring_a2(0), ring_b2(0)]
    share(part_a, 0, 0)
    share(part_b, 0, 0)
    yield
    a1.near()
    b1.near()
    for step in (-1, 1):
        seconds += [ring_a2(step), ring_b2(step)]
    for step in (-1, 1):
        share(part_a, step, 0)
        share(part_b, 0, step)
    yield
    a1.far()
    b1.far()
    seconds += [ring_a2(2), ring_b2(2)]
    share(part_a, 2, 0)
    share(part_b, 0, 2)
    yield
    for n in range(0, 8, 2):
        for ring in seconds[n : n + 2]:
            ring.near()
            for step in (-1, 1):
                share(ring.part, *ring.spot(step))
        yield
    for n in range(0, 8, 2):
        for ring in seconds[n : n + 2]:
            ring.far()
            share(ring.part, *ring.spot(2))
        if n < 6:
            yield
    yield
    crossed(len(crossing))
    for k, piece in arriving:
        recv(k, piece)
    assert counter[0] == send_sem.shape[0], counter
    yield


def device(y, zh, x, zl, c):
    return (y * 4 + zh, x * 4 + zl * 2 + c)


def advance(steps):
    next(steps, None)


def kernel(
    slots, shifts, tokens, w_qkv1, w_out1, w_qkv2, w_out2, gain1, bias1, gain2, bias2, out,
    full1, full2, staged1, staged2, zbuf1, zbuf2, tiles, frames, p_in, p_out, xw, xn, qkv, mix, mid2, snd, rbuf, ret, obuf,
    snd_one, rbuf_one, ret_one, obuf_one, wide, by_time,
    z_send, z_recv, z_local, g_send1, g_recv1, g_send2, g_recv2, e1_send, e1_recv, e1_local, m_send, m_recv,
    e2_send, e2_recv, e2_local, e3_send, e3_recv, e3_local,
):
    tm, space = lax.axis_index("tm"), lax.axis_index("space")
    y, zh = lax.div(tm, 4), lax.rem(tm, 4)
    x, zl, c = lax.div(space, 4), lax.rem(lax.div(space, 2), 2), lax.rem(space, 2)
    place = (y, zh, x, zl, c)
    sibling = device(y, zh, x, zl, 1 - c)
    video_t = lax.rem(zh + y, 4)
    is_self = video_t == x
    quarter = lax.rem(zh + 2 * zl + c, 4)
    single = quarter == 3
    pending = []

    barrier = pltpu.get_barrier_semaphore()

    def greet(target):
        pl.semaphore_signal(barrier, inc=1, device_id=target, device_id_type=MESH)

    greet(sibling)
    for step in range(1, 8):
        greet(device(y, zh, lax.rem(x + step // 2, 4), lax.rem(zl + step % 2, 2), c))

    def greet_times(n, carry):
        other = lax.rem(tm + n, 16)
        greet((other, space))
        return carry

    lax.fori_loop(1, 16, greet_times, 0)

    def greet_sources(n, carry):
        other = lax.rem(tm + lax.div(n, 2), 16)
        zl_other = lax.rem(zl + lax.rem(n, 2), 2)

        @pl.when(jnp.logical_not(is_self & (n == 0)))
        def _():
            greet((other, video_t * 4 + zl_other * 2 + c))

        return carry

    lax.fori_loop(0, 32, greet_sources, 0)
    greet(device(y, lax.rem(zh + 2 * zl + 3, 4), x, 1 - zl, c))
    stage_shard(place, w_qkv1, w_out1, staged1)
    pl.semaphore_wait(barrier, 56 - jnp.where(is_self, 1, 0))

    g1 = gather_steps(
        place, (96, 80, False), staged1, zbuf1, full1, z_send.at[0], z_recv.at[0], z_local.at[0],
        g_send1, g_recv1, pending,
    )
    g2 = gather_steps(
        place, (96, 80, False), staged2, zbuf2, full2, z_send.at[1], z_recv.at[1], z_local.at[1],
        g_send2, g_recv2, pending,
    )
    advance(g1)

    own_tile = pltpu.make_async_copy(tokens.at[zl * 4 + x], tiles.at[space], e1_local)
    own_tile.start()
    def send_tiles(steps):
        for step in steps:
            xo, zo = lax.rem(x + step // 2, 4), lax.rem(zl + step % 2, 2)
            made = pltpu.make_async_remote_copy(
                src_ref=tokens.at[zo * 4 + xo],
                dst_ref=tiles.at[space],
                send_sem=e1_send.at[step - 1],
                recv_sem=e1_recv.at[space],
                device_id=device(y, zh, xo, zo, c),
                device_id_type=MESH,
            )
            made.start()
            pending.append(made.wait_send)

    send_tiles((2, 6, 4))
    stage_shard(place, w_qkv2, w_out2, staged2)
    wide[...] = jnp.zeros_like(wide)
    frames[...] = jnp.zeros_like(frames)
    shift_r, shift_c = shifts[0, x], shifts[1, x]

    row = iota((ROWS, 1), 0)
    wc = div(row, WIN)
    spot = row - wc * WIN
    pr = div(spot, 14)
    pc = spot - 14 * pr
    r = wrap(14 * c + pr + shift_r, 28)
    col = wrap(14 * wc + pc + shift_c, 28)
    tile = 4 * div(r, 7) + div(col, 7)
    slot = jnp.zeros_like(tile)
    for s in range(16):
        slot = jnp.where(tile == slots[s], s, slot)
    index = slot * 64 + mod(r, 7) * 7 + mod(col, 7)
    p_in[...] = one_hot(jnp.where(spot < 196, index, -1), 1024)

    advance(g1)
    send_tiles((1, 3, 7, 5))

    row = iota((400, 1), 0)
    last = row >= 384
    slot8 = jnp.where(last, row - 384, div(row, 48))
    j = jnp.where(last, 48, row - 48 * slot8)
    tile = jnp.zeros_like(row)
    for n in range(8):
        tile = jnp.where(slot8 == n, slots[4 * (n // 2) + 2 * (n % 2) + c], tile)
    jr = div(j, 7)
    r = 7 * div(tile, 4) + jr
    col = 7 * mod(tile, 4) + (j - 7 * jr)
    sr = wrap(r + 28 - shift_r, 28)
    sc = wrap(col + 28 - shift_c, 28)
    wr, wc = div(sr, 14), div(sc, 14)
    index = wr * ROWS + wc * WIN + (sr - 14 * wr) * 14 + (sc - 14 * wc)
    p_out[...] = one_hot(jnp.where(slot8 < 8, index, -1), 2 * ROWS)

    advance(g1)

    own_tile.wait()

    def tile_copy(s, n):
        return pltpu.make_async_remote_copy(
            src_ref=tiles.at[s],
            dst_ref=tiles.at[s],
            send_sem=e1_send.at[7 + n],
            recv_sem=e1_recv.at[s],
            device_id=sibling,
            device_id_type=MESH,
        )

    for n, step in enumerate((0, 2, 6, 1, 3, 7, 4, 5)):
        xo, zo = lax.rem(x + step // 2, 4), lax.rem(zl + step % 2, 2)
        s = xo * 4 + zo * 2 + c
        made = tile_copy(s, n)
        if step:
            made.wait_recv()
        made.start()
        pending.append(made.wait_send)
    advance(g1)
    advance(g1)
    advance(g2)
    for step in range(8):
        s = 4 * (step // 2) + 2 * (step % 2) + 1 - c
        tile_copy(s, 0).wait_recv()

    def widen(s, carry):
        frames[s, :49, :] = tiles[s]
        return carry

    lax.fori_loop(0, 16, widen, 0)
    for first, width in PARTS:
        columns = slice(first, first + width)
        cells = frames[:, :, columns].reshape(1024, width)
        xw[:ROWS, columns] = matmul(p_in[...], cells).astype(BF16)
        advance(g1)

    def in_window(rows):
        return rows - jnp.where(rows >= WIN, WIN, 0) < 196

    normalize(xw, xn, gain1, bias1, ROWS, in_window)
    for n in range(5):
        advance(g1)
    advance(g2)
    advance(g1)
    for kind in range(3):
        project(xn, full1, qkv, kind, slice(0, ROWS))
        if kind:
            advance(g2)

    def regions(shape, axis, column):
        at = iota(shape, axis)
        down = div(at, 14)
        across = at - 14 * down
        kind = 2 * jnp.where(14 * c + down >= 28 - shift_r, 1, 0)
        kind = kind + jnp.where(14 * column + across >= 28 - shift_c, 1, 0)
        return jnp.where(at < 196, kind, -1)

    for column in range(2):
        allowed = regions((WIN, 1), 0, column) == regions((1, WIN), 1, column)
        attend(qkv, mix, pl.ds(column * WIN, WIN), allowed)
        advance(g2)

    def swap(n, core):
        first, width = PARTS[n]
        piece = mid2.at[core, :, pl.ds(first, width)]
        return pltpu.make_async_remote_copy(
            src_ref=piece,
            dst_ref=piece,
            send_sem=m_send.at[n],
            recv_sem=m_recv.at[n],
            device_id=sibling,
            device_id_type=MESH,
        )

    for n, (first, width) in enumerate(PARTS):
        mid2[c, :, first : first + width] = out_project(mix, full1, xw, slice(first, first + width), slice(0, ROWS))
        swap(n, c).start()
        pending.append(swap(n, c).wait_send)
        advance(g2)

    time = 2 * tm + zl

    def row_target(n):
        dx, dz, dh = lax.div(n, 8), lax.rem(lax.div(n, 4), 2), lax.rem(n, 4)
        xo, zo, ho = lax.rem(x + dx, 4), lax.rem(zl + dz, 2), lax.rem(zh + dh, 4)
        target = device(lax.rem(x - ho + 4, 4), ho, xo, zo, c)
        return xo * 2 + zo, lax.rem(ho + 2 * zo + c, 4), target

    def row_copy(n, part):
        s, q, target = row_target(n)
        columns = pl.ds(*PARTS[part])
        return pltpu.make_async_remote_copy(
            src_ref=snd.at[s * 3 + q, :, columns],
            dst_ref=rbuf.at[time, :, columns],
            send_sem=e2_send.at[part, n],
            recv_sem=e2_recv.at[part, time],
            device_id=target,
            device_id_type=MESH,
        )

    def one_copy(n):
        s, q, target = row_target(n)
        return pltpu.make_async_remote_copy(
            src_ref=snd_one.at[s],
            dst_ref=rbuf_one.at[time],
            send_sem=e2_send.at[1, n],
            recv_sem=e2_recv.at[1, time],
            device_id=target,
            device_id_type=MESH,
        )

    def each_row(n, part, do):
        away = jnp.logical_not(is_self & (n == 0))
        q = row_target(n)[1]

        @pl.when(away & (q < 3))
        def _():
            do(row_copy(n, part))

        if part:
            @pl.when(away & (q == 3))
            def _():
                do(one_copy(n))

    for part, (first, width) in enumerate(PARTS):
        columns = slice(first, first + width)
        swap(part, 1 - c).wait_recv()
        cells = mid2[:, :, columns].reshape(2 * ROWS, width)
        moved = matmul(p_out[...], cells)
        snd[:, :, columns] = moved[:384].astype(BF16).reshape(24, 16, width)
        for n in range(width // 128):
            wide[:8, first // 128 + n, :] = moved[384:392, 128 * n : 128 * n + 128]
        if part:
            snd_one[...] = wide[:8].astype(BF16)

        def start_rows(n, carry):
            each_row(n, part, lambda made: made.start())
            return carry

        lax.fori_loop(0, 32, start_rows, 0)

    @pl.when(is_self & jnp.logical_not(single))
    def _():
        own_rows = pltpu.make_async_copy(snd.at[(x * 2 + zl) * 3 + quarter], rbuf.at[time], e2_local)
        own_rows.start()
        own_rows.wait()

    @pl.when(is_self & single)
    def _():
        own_rows = pltpu.make_async_copy(snd_one.at[x * 2 + zl], rbuf_one.at[time], e2_local)
        own_rows.start()
        own_rows.wait()

    for n in range(8):
        advance(g2)

    row = iota((TROWS, 1), 0)
    at = div(row, 32)
    by_position = one_hot((row - 32 * at) * 16 + at, TROWS)

    row = iota((256, 1), 0)
    at = div(row, 8)
    by_time[...] = one_hot((row - 8 * at) * 32 + at, 256)

    def wait_landed(piece, part, n):
        pltpu.make_async_remote_copy(
            src_ref=piece,
            dst_ref=piece,
            send_sem=e2_send.at[part, 0],
            recv_sem=e2_recv.at[part, n],
            device_id=sibling,
            device_id_type=MESH,
        ).wait_recv()

    @pl.when(jnp.logical_not(single))
    def _():
        for part, (first, width) in enumerate(PARTS):
            columns = slice(first, first + width)

            def wait_rows(n, carry):
                @pl.when(jnp.logical_not(is_self & (n == time)))
                def _():
                    wait_landed(rbuf.at[n, :, pl.ds(first, width)], part, n)

                return carry

            lax.fori_loop(0, 32, wait_rows, 0)
            cells = rbuf[:, :, columns].reshape(TROWS, width)
            xw[:, columns] = matmul(by_position, cells).astype(BF16)

    @pl.when(single)
    def _():
        def wait_ones(n, carry):
            @pl.when(jnp.logical_not(is_self & (n == time)))
            def _():
                wait_landed(rbuf_one.at[n], 1, n)

            return carry

        lax.fori_loop(0, 32, wait_ones, 0)
        xw[...] = jnp.zeros_like(xw)
        wide[...] = rbuf_one[...].astype(F32)
        for n in range(11):
            xw[:32, 128 * n : 128 * n + 128] = wide[:, n, :].astype(BF16)

    normalize(xw, xn, gain2, bias2, TROWS, lambda rows: jnp.logical_not(single) | (rows < 32))
    advance(g2)
    def back_copy(n, half):
        other = lax.rem(tm + jnp.where(c == 0, n, 16 - n), 16)
        return pltpu.make_async_remote_copy(
            src_ref=ret.at[half, other],
            dst_ref=obuf.at[tm, half],
            send_sem=e3_send.at[half, n],
            recv_sem=e3_recv.at[half, tm],
            device_id=(other, space),
            device_id_type=MESH,
        )

    def back_one(n):
        other = lax.rem(tm + jnp.where(c == 0, n, 16 - n), 16)
        return pltpu.make_async_remote_copy(
            src_ref=ret_one.at[pl.ds(2 * other, 2)],
            dst_ref=obuf_one.at[tm],
            send_sem=e3_send.at[0, n],
            recv_sem=e3_recv.at[0, tm],
            device_id=(other, space),
            device_id_type=MESH,
        )

    def all_back(half, do):
        @pl.when(jnp.logical_not(single))
        def _():
            def one(n, carry):
                do(back_copy(n, half))
                return carry

            lax.fori_loop(1, 16, one, 0)

        if half == 0:
            @pl.when(single)
            def _():
                def one(n, carry):
                    do(back_one(n))
                    return carry

                lax.fori_loop(1, 16, one, 0)

    for half in range(2):
        part_rows = slice(256 * half, 256 * half + 256)
        for kind in range(3):
            project(xn, full2, qkv, kind, part_rows)

        def attend_group(n, carry):
            left, right = iota((128, 1), 0), iota((1, 128), 1)
            rows = pl.ds(pl.multiple_of(n * 128, 128), 128)
            attend(qkv, mix, rows, div(left, 32) == div(right, 32))
            return carry

        lax.fori_loop(2 * half, 2 * half + 2, attend_group, 0)
        for first, width in PARTS:
            columns = slice(first, first + width)
            encoded = out_project(mix, full2, xw, columns, part_rows)
            ret[half, :, :, columns] = matmul(by_time[...], encoded).astype(BF16).reshape(16, 16, width)
            if half == 0:
                for n in range(width // 128):
                    wide[:, first // 128 + n, :] = encoded[:32, 128 * n : 128 * n + 128].astype(F32)
        if half == 0:
            ret_one[...] = wide[...].astype(BF16)
        all_back(half, lambda made: made.start())

    @pl.when(jnp.logical_not(single))
    def _():
        own_back = pltpu.make_async_copy(ret.at[:, tm], obuf.at[tm], e3_local)
        own_back.start()
        own_back.wait()

    @pl.when(single)
    def _():
        own_back = pltpu.make_async_copy(ret_one.at[pl.ds(2 * tm, 2)], obuf_one.at[tm], e3_local)
        own_back.start()
        own_back.wait()

    for finish in pending:
        finish()

    for part in range(len(PARTS)):
        def finish_rows(n, carry):
            each_row(n, part, lambda made: made.wait_send())
            return carry

        lax.fori_loop(0, 32, finish_rows, 0)

    def wait_back(piece, part, n):
        pltpu.make_async_remote_copy(
            src_ref=piece,
            dst_ref=piece,
            send_sem=e3_send.at[part, 0],
            recv_sem=e3_recv.at[part, n],
            device_id=sibling,
            device_id_type=MESH,
        ).wait_recv()

    for half in range(2):
        def land(n, carry):
            q = lax.rem(lax.rem(n, 4) + 2 * zl + c, 4)

            @pl.when((n != tm) & (q < 3))
            def _():
                wait_back(obuf.at[n, half], half, n)

            if half == 0:
                @pl.when((n != tm) & (q == 3))
                def _():
                    wait_back(obuf_one.at[n], half, n)

            return carry

        lax.fori_loop(0, 16, land, 0)
    for q in range(3):
        for v in range(4):
            ho = lax.rem(q + 8 - 2 * zl - c, 4)
            n = lax.rem(v - ho + 4, 4) * 4 + ho
            early, late = obuf[n, 0].astype(F32), obuf[n, 1].astype(F32)
            for t in range(2):
                rows = jnp.concatenate([early[8 * t : 8 * t + 8], late[8 * t : 8 * t + 8]], axis=0)
                out[t, v, 16 * q : 16 * q + 16, :] = rows.astype(BF16)
    for v in range(4):
        ho = lax.rem(11 - 2 * zl - c, 4)
        n = lax.rem(v - ho + 4, 4) * 4 + ho
        for t in range(2):
            last = obuf_one[n, t].astype(F32)
            for k in range(11):
                out[t, v, 48:49, 128 * k : 128 * k + 128] = last[k : k + 1, :].astype(BF16)

    for half in range(2):
        all_back(half, lambda made: made.wait_send())


def body(
    tokens, tile_of_slot, shifts, norm_gain_space, norm_bias_space, w_qkv_space, w_out_space,
    norm_gain_time, norm_bias_time, w_qkv_time, w_out_time,
):
    smem = pl.BlockSpec(memory_space=pltpu.SMEM)
    vmem = pl.BlockSpec(memory_space=pltpu.VMEM)
    anywhere = pl.BlockSpec(memory_space=pl.ANY)
    dma = pltpu.SemaphoreType.DMA
    encoded = pl.pallas_call(
        kernel,
        out_shape=jax.ShapeDtypeStruct((2, 4, 49, D), BF16),
        in_specs=[smem, smem, anywhere] + [vmem] * 8,
        out_specs=vmem,
        scratch_shapes=[
            pltpu.VMEM((4, D, EP), BF16),
            pltpu.VMEM((4, D, EP), BF16),
            pltpu.VMEM((88, EP), BF16),
            pltpu.VMEM((88, EP), BF16),
            pltpu.VMEM((2, 88, EP), BF16),
            pltpu.VMEM((2, 88, EP), BF16),
            pltpu.VMEM((16, 49, D), BF16),
            pltpu.VMEM((16, 64, D), BF16),
            pltpu.VMEM((ROWS, 1024), BF16),
            pltpu.VMEM((400, 2 * ROWS), BF16),
            pltpu.VMEM((TROWS, D), BF16),
            pltpu.VMEM((TROWS, D), BF16),
            pltpu.VMEM((3, TROWS, EP), BF16),
            pltpu.VMEM((TROWS, EP), BF16),
            pltpu.VMEM((2, ROWS, D), BF16),
            pltpu.VMEM((24, 16, D), BF16),
            pltpu.VMEM((32, 16, D), BF16),
            pltpu.VMEM((2, 16, 16, D), BF16),
            pltpu.VMEM((16, 2, 16, D), BF16),
            pltpu.VMEM((8, 16, 128), BF16),
            pltpu.VMEM((32, 16, 128), BF16),
            pltpu.VMEM((32, 16, 128), BF16),
            pltpu.VMEM((16, 2, 16, 128), BF16),
            pltpu.VMEM((32, 16, 128), F32),
            pltpu.VMEM((256, 256), BF16),
            dma((2, 3)), dma((2, 2)), dma((2,)), dma((COPIES[0],)), dma((COPIES[0],)), dma((COPIES[1],)), dma((COPIES[1],)),
            dma((15,)), dma((16,)), dma, dma((2,)), dma((2,)),
            dma((2, 32)), dma((2, 32)), dma, dma((2, 16)), dma((2, 16)), dma,
        ],
        compiler_params=pltpu.CompilerParams(
            collective_id=0, has_side_effects=True, vmem_limit_bytes=60 * 1024 * 1024
        ),
        cost_estimate=pl.CostEstimate(flops=12_000_000_000, bytes_accessed=40_000_000, transcendentals=2_000_000),
    )(
        tile_of_slot, shifts.T, tokens.reshape(8, 49, D), w_qkv_space, w_out_space.T, w_qkv_time, w_out_time.T,
        norm_gain_space, norm_bias_space, norm_gain_time, norm_bias_time,
    )
    return encoded.reshape(tokens.shape)


def solution(mesh):
    placed = (
        P("tm", "space", None, None, None), P(), P(), P(), P(), P("tm", None), P(None, "tm"),
        P(), P(), P("tm", None), P(None, "tm"),
    )
    return jax.shard_map(
        body,
        mesh=mesh,
        in_specs=placed,
        out_specs=P("tm", "space", None, None, None),
        check_vma=False,
    )
```
